128 devices in a mesh: dom: 128 (over x, z, y, core).
Axes of the slice: x: 4, y: 4, z: 4, core: 2. Of those that a mesh axis runs over, the one named last changes fastest.
Arguments:
- feats: bfloat16 [262144, 256], P('dom'), may hold values from -6 to 6
- hub_feat: bfloat16 [16384, 256], P('dom'), may hold values from -6 to 6
- weight: bfloat16 [512, 256], replicated, may hold values from -0.25 to 0.25
- bias: float32 [256], replicated, may hold values from -4 to 4
- loc_nbr: int32 [262144, 16], P('dom'), may hold values from 0 to 2047
- loc_len: int32 [262144], P('dom'), may hold values from 1 to 16
- hub_nbr: int32 [262144, 8], P('dom'), may hold values from 0 to 16383
- hub_len: int32 [262144], P('dom'), may hold values from 0 to 8
- send_list: int32 [16384, 64], P('dom'), may hold values from 0 to 2047
- halo_nbr: int32 [262144, 8], P('dom'), may hold values from 0 to 8191
- halo_len: int32 [262144], P('dom'), may hold values from 0 to 8
Outputs:
- layer_out: bfloat16 [262144, 256], P('dom')
The draws below stay inside these ranges and needn't reach their ends.
All inputs are finite; a program needn't handle non-finite values.
Results may differ from the reference program's by a relative error of at most 0.0016.
Values may be sent and summed in bfloat16 or wider, within the bound.
No kernel may reach another device: no remote copies, remote signals or barrier semaphores. Data moves between devices by JAX's collectives and lax.ppermute only.
A program may use at most 128 MiB of HBM per device.

```python
import jax
import jax.numpy as jnp
from jax import lax

H = 256
ROWS = 2048
SLOTS = 64
K_LOC = 16
K_HUB = 8
K_HALO = 8
NODES = 262144
HUBS = 16384
N_DOM = 128


def pair_counts(key):
    inner = jax.random.fold_in(key, 11)
    base = jax.random.randint(jax.random.fold_in(inner, 1), (N_DOM * N_DOM,), 1, SLOTS + 1)
    heavy = jax.random.randint(jax.random.fold_in(inner, 2), (N_DOM,), 0, 4) == 0
    target = jnp.arange(N_DOM * N_DOM, dtype=jnp.int32) % N_DOM
    counts = jnp.where(heavy[target], SLOTS, base)
    return counts.at[(N_DOM - 1) * N_DOM].set(SLOTS).astype(jnp.int32)


def draw_halo_nbr(key, part):
    counts = pair_counts(key)
    key = jax.random.fold_in(key, 5)
    source = jax.random.randint(jax.random.fold_in(key, 1), (NODES, K_HALO), 0, N_DOM)
    target = (jnp.arange(NODES, dtype=jnp.int32) // ROWS)[:, None]
    limit = counts[source * N_DOM + target]
    raw = jax.random.randint(jax.random.fold_in(key, 2), (NODES, K_HALO), 0, 1048576)
    result = (source * SLOTS + raw % limit).astype(jnp.int32)
    result = result.at[0, 0].set(N_DOM * SLOTS - 1)
    return result.at[1, 0].set(0).astype(jnp.int32)


def plant(values, stream_key, smallest, high):
    spot = [jax.random.randint(jax.random.fold_in(stream_key, axis), (), 0, length) for axis, length in enumerate(values.shape)]
    longest = values.shape.index(max(values.shape))
    beside = spot[:longest] + [(spot[longest] + 1) % values.shape[longest]] + spot[longest + 1:]
    return values.at[tuple(spot)].set(smallest).at[tuple(beside)].set(high)


def level_of(rng, extent, cuts, smallest, high):
    level = 1.0
    for position, blocks in cuts:
        heights = jax.random.uniform(jax.random.fold_in(jax.random.fold_in(rng, 6), position), (blocks,), jnp.float32, smallest / len(cuts), high / len(cuts))
        level = level * jnp.repeat(jnp.exp(heights), extent[position] // blocks).reshape((-1,) + (1,) * (len(extent) - 1 - position))
    return level


def noise(rng, shape, scale, most, shards=(), kind=jnp.bfloat16):
    drawn = scale * jax.random.normal(rng, shape, jnp.float32)
    if shards:
        drawn = drawn * level_of(rng, shape, shards, -0.22, 0.18)
    return jnp.clip(drawn, -most, most).astype(kind)


def setup_inputs(seed: int = 0) -> dict:
    key_list = jax.random.split(jax.random.key(seed), 12)
    feats = noise(key_list[0], (NODES, H), 1.0, 6.0, ((0, 128),))
    hub_feat = noise(key_list[1], (HUBS, H), 1.0, 6.0, ((0, 128),))
    weight = noise(key_list[2], (2 * H, H), (2 * H) ** -0.5, 0.25)
    bias = noise(key_list[3], (H,), 1.0, 4.0, (), jnp.float32)
    loc_nbr = plant(jax.random.randint(key_list[4], (NODES, K_LOC), 0, ROWS), jax.random.fold_in(key_list[4], 1), 0, ROWS - 1).astype(jnp.int32)
    loc_len = plant(jax.random.randint(key_list[5], (NODES,), 1, K_LOC + 1), jax.random.fold_in(key_list[5], 1), 1, K_LOC).astype(jnp.int32)
    hub_nbr = plant(jax.random.randint(key_list[6], (NODES, K_HUB), 0, HUBS), jax.random.fold_in(key_list[6], 1), 0, HUBS - 1).astype(jnp.int32)
    hub_len = plant(jax.random.randint(key_list[7], (NODES,), 0, K_HUB + 1), jax.random.fold_in(key_list[7], 1), 0, K_HUB).astype(jnp.int32)
    send_list = plant(jax.random.randint(key_list[8], (N_DOM * N_DOM, SLOTS), 0, ROWS), jax.random.fold_in(key_list[8], 1), 0, ROWS - 1).astype(jnp.int32)
    halo_nbr = draw_halo_nbr(jax.random.fold_in(key_list[11], 71), 0)
    halo_len = plant(jax.random.randint(key_list[10], (NODES,), 0, K_HALO + 1), jax.random.fold_in(key_list[10], 1), 0, K_HALO).astype(jnp.int32)
    return dict(feats=feats, hub_feat=hub_feat, weight=weight, bias=bias, loc_nbr=loc_nbr, loc_len=loc_len, hub_nbr=hub_nbr, hub_len=hub_len, send_list=send_list, halo_nbr=halo_nbr, halo_len=halo_len)


def masked_sum(rows, length):
    mask = jnp.arange(rows.shape[1], dtype=jnp.int32)[None, :] < length[:, None]
    return jnp.sum(rows.astype(jnp.float32) * mask[:, :, None].astype(jnp.float32), axis=1)


def reference(feats, hub_feat, weight, bias, loc_nbr, loc_len, hub_nbr, hub_len, send_list, halo_nbr, halo_len):
    def one_device(owner):
        start = (owner * ROWS).astype(jnp.int32)
        own_rows = lax.dynamic_slice_in_dim(feats, start, ROWS, 0)
        loc_idx = lax.dynamic_slice_in_dim(loc_nbr, start, ROWS, 0)
        loc_cnt = lax.dynamic_slice_in_dim(loc_len, start, ROWS, 0)
        hub_idx = lax.dynamic_slice_in_dim(hub_nbr, start, ROWS, 0)
        hub_cnt = lax.dynamic_slice_in_dim(hub_len, start, ROWS, 0)
        halo_idx = lax.dynamic_slice_in_dim(halo_nbr, start, ROWS, 0)
        halo_cnt = lax.dynamic_slice_in_dim(halo_len, start, ROWS, 0)
        loc_sum = masked_sum(own_rows[loc_idx], loc_cnt)
        hub_sum = masked_sum(hub_feat[hub_idx], hub_cnt)
        source = halo_idx // SLOTS
        slot = halo_idx % SLOTS
        local_row = send_list[source * N_DOM + owner, slot]
        halo_sum = masked_sum(feats[(source * ROWS + local_row).astype(jnp.int32)], halo_cnt)
        degree = (loc_cnt + hub_cnt + halo_cnt).astype(jnp.float32)
        agg = ((loc_sum + hub_sum + halo_sum) / degree[:, None]).astype(jnp.bfloat16)
        joined = jnp.concatenate([own_rows, agg], axis=1)
        result = jnp.dot(joined, weight, preferred_element_type=jnp.float32) + bias
        return jnp.maximum(result, 0.0).astype(jnp.bfloat16)

    blocks = lax.map(one_device, jnp.arange(N_DOM, dtype=jnp.int32))
    return blocks.reshape(NODES, H)
```

```python
import jax
import jax.numpy as jnp
from jax import lax
from jax.experimental import pallas as pl
from jax.experimental.pallas import tpu as pltpu
from jax.sharding import PartitionSpec as P

LANES = 128
VMEM_LIMIT = 48 * 2**20


def one_hot(mask):
    return jnp.where(mask, 1.0, 0.0).astype(jnp.bfloat16)


def send_body(list_ref, feats_ref, out_ref, hot_ref):
    columns = list_ref[...].T
    rows = feats_ref.shape[0]
    lane = lax.broadcasted_iota(jnp.int32, (LANES, LANES), 1)
    for j in range(columns.shape[1]):
        wanted = jnp.broadcast_to(columns[:, j : j + 1], (LANES, LANES))
        for t in range(rows // LANES):
            hot_ref[j * LANES : (j + 1) * LANES, t * LANES : (t + 1) * LANES] = one_hot(
                wanted == lane + t * LANES
            )
    out_ref[...] = jnp.dot(
        hot_ref[...], feats_ref[...], preferred_element_type=jnp.float32
    ).astype(out_ref.dtype)


def gather_to_send(feats, send_list):
    rows, width = feats.shape
    count = send_list.size
    group = 8 * LANES
    return pl.pallas_call(
        send_body,
        grid=(count // group,),
        in_specs=[
            pl.BlockSpec((8, LANES), lambda i: (i, 0)),
            pl.BlockSpec((rows, width), lambda i: (0, 0)),
        ],
        out_specs=pl.BlockSpec((group, width), lambda i: (i, 0)),
        out_shape=jax.ShapeDtypeStruct((count, width), feats.dtype),
        scratch_shapes=[pltpu.VMEM((group, rows), jnp.bfloat16)],
        compiler_params=pltpu.CompilerParams(vmem_limit_bytes=VMEM_LIMIT),
        cost_estimate=pl.CostEstimate(
            flops=2 * count * rows * width, bytes_accessed=2 * count * width, transcendentals=0
        ),
        name="gather_to_send",
    )(send_list.reshape(count // LANES, LANES), feats)


def local_body(part, high_ref, low_ref, feats_ref, out_ref, count_ref):
    rows = feats_ref.shape[0]
    blocks = rows // LANES
    groups, contract = high_ref.shape
    tall = lax.broadcasted_iota(jnp.int32, (blocks * part, contract), 0)
    short = lax.broadcasted_iota(jnp.int32, (LANES, contract), 0)
    for g in range(groups):
        left = one_hot(tall == high_ref[g : g + 1, :])
        right = one_hot(short == low_ref[g : g + 1, :])
        counts = lax.dot_general(
            left, right, (((1,), (1,)), ((), ())), preferred_element_type=jnp.float32
        ).astype(jnp.bfloat16)
        for b in range(blocks):
            count_ref[g * part : (g + 1) * part, b * LANES : (b + 1) * LANES] = counts[
                b * part : (b + 1) * part, :
            ]
    out_ref[...] = jnp.dot(count_ref[...], feats_ref[...], preferred_element_type=jnp.float32)


def local_sums(feats, neighbours, length):
    rows, width = feats.shape
    slots = neighbours.shape[1]
    part = 2 * LANES // slots
    used = jnp.arange(slots, dtype=jnp.int32)[None, :] < length[:, None]
    place = (jnp.arange(rows, dtype=jnp.int32) % part)[:, None]
    high = jnp.where(used, (neighbours // LANES) * part + place, -1).reshape(-1, part * slots)
    low = (neighbours % LANES).reshape(-1, part * slots)
    groups = 16
    return pl.pallas_call(
        lambda *refs: local_body(part, *refs),
        grid=(rows // (groups * part),),
        in_specs=[
            pl.BlockSpec((groups, part * slots), lambda i: (i, 0)),
            pl.BlockSpec((groups, part * slots), lambda i: (i, 0)),
            pl.BlockSpec((rows, width), lambda i: (0, 0)),
        ],
        out_specs=pl.BlockSpec((groups * part, width), lambda i: (i, 0)),
        out_shape=jax.ShapeDtypeStruct((rows, width), jnp.float32),
        scratch_shapes=[pltpu.VMEM((groups * part, rows), jnp.bfloat16)],
        compiler_params=pltpu.CompilerParams(vmem_limit_bytes=VMEM_LIMIT),
        cost_estimate=pl.CostEstimate(
            flops=4 * rows * rows * width, bytes_accessed=4 * rows * width, transcendentals=0
        ),
        name="local_sums",
    )(high, low, feats)


def load_table(source, stage, table, sem):
    count = source.shape[0]
    size = stage.shape[0] // stage_chunks(count)
    chunks = stage_chunks(count)

    def copy(c):
        span = pl.ds(c * size, size)
        return pltpu.make_async_copy(source.at[span], stage.at[span], sem.at[c])

    for c in range(chunks):
        copy(c).start()
    table[2 * count : 2 * count + 8, :] = jnp.zeros((8, LANES), jnp.float32)
    for c in range(chunks):
        copy(c).wait()

        def widen(i, carry, c=c):
            start = c * size + i * 256
            block = stage[pl.ds(pl.multiple_of(start, 256), 256), :].astype(jnp.float32)
            table[pl.ds(2 * start, 256, stride=2), :] = block[:, :LANES]
            table[pl.ds(2 * start + 1, 256, stride=2), :] = block[:, LANES:]
            return carry

        lax.fori_loop(0, size // 256, widen, 0)


def stage_chunks(count):
    return 4


def add_rows(index_ref, table, out_ref, slots, unroll):
    def step(i, carry):
        for u in range(unroll):
            v = i * unroll + u
            total = None
            for k in range(slots):
                row = table[pl.ds(pl.multiple_of(index_ref[v * slots + k], 2), 2), :]
                total = row if total is None else total + row
            out_ref[pl.ds(pl.multiple_of(2 * v, 2), 2), :] = total
        return carry

    lax.fori_loop(0, out_ref.shape[0] // (2 * unroll), step, 0)


def hub_body(slots, index_ref, source, out_ref, stage, table, sem):
    load_table(source, stage, table, sem)
    add_rows(index_ref, table, out_ref, slots, 16)


def row_index(neighbours, length, count):
    used = jnp.arange(neighbours.shape[1], dtype=jnp.int32)[None, :] < length[:, None]
    return jnp.where(used, neighbours * 2, 2 * count).reshape(-1)


def hub_sums(index, slots, source):
    count, width = source.shape
    rows = index.shape[0] // slots
    return pl.pallas_call(
        lambda *refs: hub_body(slots, *refs),
        in_specs=[
            pl.BlockSpec(memory_space=pltpu.SMEM),
            pl.BlockSpec(memory_space=pl.ANY),
        ],
        out_specs=pl.BlockSpec(memory_space=pltpu.VMEM),
        out_shape=jax.ShapeDtypeStruct((2 * rows, LANES), jnp.float32),
        scratch_shapes=[
            pltpu.VMEM((count, width), source.dtype),
            pltpu.VMEM((2 * count + 8, LANES), jnp.float32),
            pltpu.SemaphoreType.DMA((stage_chunks(count),)),
        ],
        compiler_params=pltpu.CompilerParams(vmem_limit_bytes=VMEM_LIMIT),
        cost_estimate=pl.CostEstimate(
            flops=40_000_000_000, bytes_accessed=2 * count * width, transcendentals=0
        ),
        name="hub_sums",
    )(index, source)


def layer_body(
    slots, index_ref, source, hub_ref, loc_ref, degree_ref, feats_ref, weight_ref, bias_ref,
    out_ref, stage, table, halo, sem,
):
    load_table(source, stage, table, sem)
    add_rows(index_ref, table, halo, slots, 16)
    rows, width = feats_ref.shape
    tile = 256

    def finish(i, carry):
        start = pl.multiple_of(i * tile, tile)
        span = pl.ds(start, tile)
        degree = degree_ref[span, :]
        halves = []
        for h in range(2):
            pick = pl.ds(2 * start + h, tile, stride=2)
            total = loc_ref[span, h * LANES : (h + 1) * LANES] + hub_ref[pick, :] + halo[pick, :]
            halves.append((total / degree).astype(jnp.bfloat16))
        agg = jnp.concatenate(halves, axis=1)
        result = jnp.dot(
            feats_ref[span, :], weight_ref[:width, :], preferred_element_type=jnp.float32
        )
        result += jnp.dot(agg, weight_ref[width:, :], preferred_element_type=jnp.float32)
        result += bias_ref[...]
        out_ref[span, :] = jnp.maximum(result, 0.0).astype(out_ref.dtype)
        return carry

    lax.fori_loop(0, rows // tile, finish, 0)


def layer(index, slots, source, hub, loc, degree, feats, weight, bias):
    count, width = source.shape
    rows = feats.shape[0]
    vmem = pl.BlockSpec(memory_space=pltpu.VMEM)
    return pl.pallas_call(
        lambda *refs: layer_body(slots, *refs),
        in_specs=[
            pl.BlockSpec(memory_space=pltpu.SMEM),
            pl.BlockSpec(memory_space=pl.ANY),
            vmem, vmem, vmem, vmem, vmem, vmem,
        ],
        out_specs=vmem,
        out_shape=jax.ShapeDtypeStruct((rows, width), feats.dtype),
        scratch_shapes=[
            pltpu.VMEM((count, width), source.dtype),
            pltpu.VMEM((2 * count + 8, LANES), jnp.float32),
            pltpu.VMEM((2 * rows, LANES), jnp.float32),
            pltpu.SemaphoreType.DMA((stage_chunks(count),)),
        ],
        compiler_params=pltpu.CompilerParams(vmem_limit_bytes=VMEM_LIMIT),
        cost_estimate=pl.CostEstimate(
            flops=40_000_000_000, bytes_accessed=2 * count * width, transcendentals=0
        ),
        name="layer",
    )(index, source, hub, loc, degree, feats, weight, bias)


def per_device(
    feats, hub_feat, weight, bias, loc_nbr, loc_len, hub_nbr, hub_len, send_list, halo_nbr, halo_len
):
    rows, width = feats.shape
    peers, slots = send_list.shape
    whole_hubs = lax.all_gather(hub_feat, "dom", axis=0, tiled=True)
    outgoing = gather_to_send(feats, send_list)
    arrived = lax.all_to_all(
        outgoing.reshape(peers, slots, width), "dom", split_axis=0, concat_axis=0, tiled=True
    ).reshape(peers * slots, width)
    loc = local_sums(feats, loc_nbr, loc_len)
    hub = hub_sums(row_index(hub_nbr, hub_len, whole_hubs.shape[0]), hub_nbr.shape[1], whole_hubs)
    degree = jnp.broadcast_to(
        (loc_len + hub_len + halo_len).astype(jnp.float32)[:, None], (rows, LANES)
    )
    return layer(
        row_index(halo_nbr, halo_len, peers * slots),
        halo_nbr.shape[1],
        arrived,
        hub,
        loc,
        degree,
        feats,
        weight,
        bias[None, :],
    )


def solution(mesh):
    placed = (
        P("dom", None),
        P("dom", None),
        P(),
        P(),
        P("dom", None),
        P("dom"),
        P("dom", None),
        P("dom"),
        P("dom", None),
        P("dom", None),
        P("dom"),
    )
    return jax.shard_map(
        per_device, mesh=mesh, in_specs=placed, out_specs=P("dom", None), check_vma=False
    )
```

```python
import jax
import jax.numpy as jnp
from jax import lax
from jax.experimental import pallas as pl
from jax.experimental.pallas import tpu as pltpu
from jax.sharding import PartitionSpec as P

LANES = 128
VMEM_LIMIT = 48 * 2**20
CHUNK = 2048
WIDEN = 256


def one_hot(mask):
    return jnp.where(mask, 1.0, 0.0).astype(jnp.bfloat16)


def send_body(list_ref, feats_ref, out_ref, hot_ref):
    columns = list_ref[...].T
    rows = feats_ref.shape[0]
    lane = lax.broadcasted_iota(jnp.int32, (LANES, LANES), 1)
    for j in range(columns.shape[1]):
        wanted = jnp.broadcast_to(columns[:, j : j + 1], (LANES, LANES))
        for t in range(rows // LANES):
            hot_ref[j * LANES : (j + 1) * LANES, t * LANES : (t + 1) * LANES] = one_hot(
                wanted == lane + t * LANES
            )
    out_ref[...] = jnp.dot(
        hot_ref[...], feats_ref[...], preferred_element_type=jnp.float32
    ).astype(out_ref.dtype)


def gather_to_send(feats, send_list):
    rows, width = feats.shape
    count = send_list.size
    group = 8 * LANES
    return pl.pallas_call(
        send_body,
        grid=(count // group,),
        in_specs=[
            pl.BlockSpec((8, LANES), lambda i: (i, 0)),
            pl.BlockSpec((rows, width), lambda i: (0, 0)),
        ],
        out_specs=pl.BlockSpec((group, width), lambda i: (i, 0)),
        out_shape=jax.ShapeDtypeStruct((count, width), feats.dtype),
        scratch_shapes=[pltpu.VMEM((group, rows), jnp.bfloat16)],
        compiler_params=pltpu.CompilerParams(vmem_limit_bytes=VMEM_LIMIT),
        cost_estimate=pl.CostEstimate(
            flops=2 * count * rows * width, bytes_accessed=2 * count * width, transcendentals=0
        ),
        name="gather_to_send",
    )(send_list.reshape(count // LANES, LANES), feats)


def local_body(part, high_ref, low_ref, feats_ref, out_ref, count_ref):
    rows = feats_ref.shape[0]
    blocks = rows // LANES
    groups, contract = high_ref.shape
    tall = lax.broadcasted_iota(jnp.int32, (blocks * part, contract), 0)
    short = lax.broadcasted_iota(jnp.int32, (LANES, contract), 0)
    for g in range(groups):
        left = one_hot(tall == high_ref[g : g + 1, :])
        right = one_hot(short == low_ref[g : g + 1, :])
        counts = lax.dot_general(
            left, right, (((1,), (1,)), ((), ())), preferred_element_type=jnp.float32
        ).astype(jnp.bfloat16)
        for b in range(blocks):
            count_ref[g * part : (g + 1) * part, b * LANES : (b + 1) * LANES] = counts[
                b * part : (b + 1) * part, :
            ]
    out_ref[...] = jnp.dot(count_ref[...], feats_ref[...], preferred_element_type=jnp.float32)


def local_sums(feats, neighbours, length):
    rows, width = feats.shape
    slots = neighbours.shape[1]
    part = 2 * LANES // slots
    used = jnp.arange(slots, dtype=jnp.int32)[None, :] < length[:, None]
    place = (jnp.arange(rows, dtype=jnp.int32) % part)[:, None]
    high = jnp.where(used, (neighbours // LANES) * part + place, -1).reshape(-1, part * slots)
    low = (neighbours % LANES).reshape(-1, part * slots)
    groups = 16
    return pl.pallas_call(
        lambda *refs: local_body(part, *refs),
        grid=(rows // (groups * part),),
        in_specs=[
            pl.BlockSpec((groups, part * slots), lambda i: (i, 0)),
            pl.BlockSpec((groups, part * slots), lambda i: (i, 0)),
            pl.BlockSpec((rows, width), lambda i: (0, 0)),
        ],
        out_specs=pl.BlockSpec((groups * part, width), lambda i: (i, 0)),
        out_shape=jax.ShapeDtypeStruct((rows, width), jnp.float32),
        scratch_shapes=[pltpu.VMEM((groups * part, rows), jnp.bfloat16)],
        compiler_params=pltpu.CompilerParams(vmem_limit_bytes=VMEM_LIMIT),
        cost_estimate=pl.CostEstimate(
            flops=4 * rows * rows * width, bytes_accessed=4 * rows * width, transcendentals=0
        ),
        name="local_sums",
    )(high, low, feats)


def load_table(sources, stage, table, sem):
    copies = []
    start = 0
    for source in sources:
        count = source.shape[0]
        size = min(count, CHUNK)
        for first in range(0, count, size):
            copies.append(
                pltpu.make_async_copy(
                    source.at[pl.ds(first, size)],
                    stage.at[pl.ds(start, size)],
                    sem.at[len(copies)],
                )
            )
            start += size
    for copy in copies:
        copy.start()
    table[2 * start : 2 * start + 8, :] = jnp.zeros((8, LANES), jnp.float32)
    start = 0
    for copy in copies:
        copy.wait()
        size = copy.dst_ref.shape[0]

        def widen(i, carry, first=start):
            at = first + i * WIDEN
            block = stage[pl.ds(pl.multiple_of(at, WIDEN), WIDEN), :].astype(jnp.float32)
            table[pl.ds(2 * at, WIDEN, stride=2), :] = block[:, :LANES]
            table[pl.ds(2 * at + 1, WIDEN, stride=2), :] = block[:, LANES:]
            return carry

        lax.fori_loop(0, size // WIDEN, widen, 0)
        start += size


def chunk_count(sources):
    return sum(-(-source.shape[0] // CHUNK) for source in sources)


def add_rows(index_ref, table, out_ref, slots, unroll):
    def step(i, carry):
        for u in range(unroll):
            v = i * unroll + u
            total = None
            for k in range(slots):
                row = table[pl.ds(pl.multiple_of(index_ref[v * slots + k], 2), 2), :]
                total = row if total is None else total + row
            out_ref[pl.ds(pl.multiple_of(2 * v, 2), 2), :] = total
        return carry

    lax.fori_loop(0, out_ref.shape[0] // (2 * unroll), step, 0)


def hub_body(slots, pieces, index_ref, *refs):
    sources, (out_ref, stage, table, sem) = refs[:pieces], refs[pieces:]
    load_table(sources, stage, table, sem)
    add_rows(index_ref, table, out_ref, slots, 16)


def row_index(neighbours, length, count):
    used = jnp.arange(neighbours.shape[1], dtype=jnp.int32)[None, :] < length[:, None]
    return jnp.where(used, neighbours * 2, 2 * count).reshape(-1)


def hub_sums(index, slots, sources):
    width = sources[0].shape[1]
    count = sum(source.shape[0] for source in sources)
    rows = index.shape[0] // slots
    return pl.pallas_call(
        lambda *refs: hub_body(slots, len(sources), *refs),
        in_specs=[pl.BlockSpec(memory_space=pltpu.SMEM)]
        + [pl.BlockSpec(memory_space=pl.ANY)] * len(sources),
        out_specs=pl.BlockSpec(memory_space=pltpu.VMEM),
        out_shape=jax.ShapeDtypeStruct((2 * rows, LANES), jnp.float32),
        scratch_shapes=[
            pltpu.VMEM((count, width), sources[0].dtype),
            pltpu.VMEM((2 * count + 8, LANES), jnp.float32),
            pltpu.SemaphoreType.DMA((chunk_count(sources),)),
        ],
        compiler_params=pltpu.CompilerParams(vmem_limit_bytes=VMEM_LIMIT),
        cost_estimate=pl.CostEstimate(
            flops=20_000_000_000, bytes_accessed=2 * count * width, transcendentals=0
        ),
        name="hub_sums",
    )(index, *sources)


def layer_body(
    slots, index_ref, source, hub_ref, loc_ref, degree_ref, feats_ref, weight_ref, bias_ref,
    out_ref, stage, table, halo, sem,
):
    load_table([source], stage, table, sem)
    add_rows(index_ref, table, halo, slots, 16)
    rows, width = feats_ref.shape
    tile = 256

    def finish(i, carry):
        start = pl.multiple_of(i * tile, tile)
        span = pl.ds(start, tile)
        degree = degree_ref[span, :]
        halves = []
        for h in range(2):
            pick = pl.ds(2 * start + h, tile, stride=2)
            total = loc_ref[span, h * LANES : (h + 1) * LANES] + hub_ref[pick, :] + halo[pick, :]
            halves.append((total / degree).astype(jnp.bfloat16))
        agg = jnp.concatenate(halves, axis=1)
        result = jnp.dot(
            feats_ref[span, :], weight_ref[:width, :], preferred_element_type=jnp.float32
        )
        result += jnp.dot(agg, weight_ref[width:, :], preferred_element_type=jnp.float32)
        result += bias_ref[...]
        out_ref[span, :] = jnp.maximum(result, 0.0).astype(out_ref.dtype)
        return carry

    lax.fori_loop(0, rows // tile, finish, 0)


def layer(index, slots, source, hub, loc, degree, feats, weight, bias):
    count, width = source.shape
    rows = feats.shape[0]
    vmem = pl.BlockSpec(memory_space=pltpu.VMEM)
    return pl.pallas_call(
        lambda *refs: layer_body(slots, *refs),
        in_specs=[
            pl.BlockSpec(memory_space=pltpu.SMEM),
            pl.BlockSpec(memory_space=pl.ANY),
            vmem, vmem, vmem, vmem, vmem, vmem,
        ],
        out_specs=vmem,
        out_shape=jax.ShapeDtypeStruct((rows, width), feats.dtype),
        scratch_shapes=[
            pltpu.VMEM((count, width), source.dtype),
            pltpu.VMEM((2 * count + 8, LANES), jnp.float32),
            pltpu.VMEM((2 * rows, LANES), jnp.float32),
            pltpu.SemaphoreType.DMA((chunk_count([source]),)),
        ],
        compiler_params=pltpu.CompilerParams(vmem_limit_bytes=VMEM_LIMIT),
        cost_estimate=pl.CostEstimate(
            flops=40_000_000_000, bytes_accessed=2 * count * width, transcendentals=0
        ),
        name="layer",
    )(index, source, hub, loc, degree, feats, weight, bias)


RING = 4
STRIDES = {"x": 32, "z": 8, "y": 2}
ORDERS = (("y", "z", "x"), ("z", "x", "y"))


def moved(stage, step):
    pairs = []
    for device in range(2 * RING**3):
        stride = STRIDES[ORDERS[device % 2][stage]]
        at = device // stride % RING
        pairs.append((device, device + (step(at) - at) * stride))
    return pairs


def gather_hubs(own):
    block = own
    for stage in range(2):
        for flip in (1, 3):
            other = lax.ppermute(block, "dom", moved(stage, lambda i, flip=flip: i ^ flip))
            block = jnp.concatenate([block, other], axis=0)
    blocks = [block]
    for shift in (1, 3, 2):
        blocks.append(
            lax.ppermute(block, "dom", moved(2, lambda i, shift=shift: (i - shift) % RING))
        )
    swap = [(device, device ^ 1) for device in range(2 * RING**3)]
    return blocks + [lax.ppermute(part, "dom", swap) for part in blocks]


def gray(value):
    return value ^ (value >> 1)


def hub_place(hub, rows_each):
    me = lax.axis_index("dom")
    device = hub // rows_each
    apart = {
        name: ((device // stride % RING), (me // stride % RING)) for name, stride in STRIDES.items()
    }
    near = {name: gray(theirs ^ mine) for name, (theirs, mine) in apart.items()}
    far = {name: gray((theirs - mine) & (RING - 1)) for name, (theirs, mine) in apart.items()}
    core = device & 1

    def place(order):
        return (far[order[2]] * RING + near[order[1]]) * RING + near[order[0]]

    block = jnp.where(core == 0, place(ORDERS[0]), place(ORDERS[1]))
    block += (core ^ (me & 1)) * RING**3
    return block * rows_each + hub % rows_each


def per_device(
    feats, hub_feat, weight, bias, loc_nbr, loc_len, hub_nbr, hub_len, send_list, halo_nbr, halo_len
):
    rows, width = feats.shape
    peers, slots = send_list.shape
    hubs = gather_hubs(hub_feat)
    outgoing = gather_to_send(feats, send_list)
    arrived = lax.all_to_all(
        outgoing.reshape(peers, slots, width), "dom", split_axis=0, concat_axis=0, tiled=True
    ).reshape(peers * slots, width)
    loc = local_sums(feats, loc_nbr, loc_len)
    each = hub_feat.shape[0]
    hub_index = row_index(hub_place(hub_nbr, each), hub_len, lax.axis_size("dom") * each)
    hub = hub_sums(hub_index, hub_nbr.shape[1], hubs)
    degree = jnp.broadcast_to(
        (loc_len + hub_len + halo_len).astype(jnp.float32)[:, None], (rows, LANES)
    )
    return layer(
        row_index(halo_nbr, halo_len, peers * slots),
        halo_nbr.shape[1],
        arrived,
        hub,
        loc,
        degree,
        feats,
        weight,
        bias[None, :],
    )


def solution(mesh):
    placed = (
        P("dom", None),
        P("dom", None),
        P(),
        P(),
        P("dom", None),
        P("dom"),
        P("dom", None),
        P("dom"),
        P("dom", None),
        P("dom", None),
        P("dom"),
    )
    return jax.shard_map(
        per_device, mesh=mesh, in_specs=placed, out_specs=P("dom", None), check_vma=False
    )
```

```python
import jax
import jax.numpy as jnp
from jax import lax
from jax.experimental import pallas as pl
from jax.experimental.pallas import tpu as pltpu
from jax.sharding import PartitionSpec as P

LANES = 128
MIB = 2**20
CHUNK = 1024
WIDEN = 256
UNROLL = 32


def one_hot(mask):
    return jnp.where(mask, 1.0, 0.0).astype(jnp.bfloat16)


def send_body(list_ref, feats_ref, out_ref, hot_ref):
    columns = list_ref[...].T
    rows = feats_ref.shape[0]
    lane = lax.broadcasted_iota(jnp.int32, (LANES, LANES), 1)
    for j in range(columns.shape[1]):
        wanted = jnp.broadcast_to(columns[:, j : j + 1], (LANES, LANES))
        for t in range(rows // LANES):
            hot_ref[j * LANES : (j + 1) * LANES, t * LANES : (t + 1) * LANES] = one_hot(
                wanted == lane + t * LANES
            )
    out_ref[...] = jnp.dot(
        hot_ref[...], feats_ref[...], preferred_element_type=jnp.float32
    ).astype(out_ref.dtype)


def gather_to_send(feats, send_list, piece, pieces, so_far):
    rows, width = feats.shape
    count = send_list.size
    group = 8 * LANES
    steps = count // group // pieces
    first = piece * steps
    inputs = [send_list.reshape(count // LANES, LANES), feats]
    in_specs = [
        pl.BlockSpec((8, LANES), lambda i: (first + i, 0)),
        pl.BlockSpec((rows, width), lambda i: (0, 0)),
    ]
    aliases = {}
    if so_far is not None:
        inputs.append(so_far)
        in_specs.append(pl.BlockSpec(memory_space=pl.ANY))
        aliases = {2: 0}
    return pl.pallas_call(
        lambda list_ref, feats_ref, *refs: send_body(list_ref, feats_ref, refs[-2], refs[-1]),
        grid=(steps,),
        in_specs=in_specs,
        out_specs=pl.BlockSpec((group, width), lambda i: (first + i, 0)),
        out_shape=jax.ShapeDtypeStruct((count, width), feats.dtype),
        scratch_shapes=[pltpu.VMEM((group, rows), jnp.bfloat16)],
        input_output_aliases=aliases,
        compiler_params=pltpu.CompilerParams(vmem_limit_bytes=14 * MIB),
        cost_estimate=pl.CostEstimate(
            flops=4 * count * rows * width // pieces,
            bytes_accessed=2 * count * width // pieces,
            transcendentals=0,
        ),
        name="gather_to_send",
    )(*inputs)


def local_body(part, code_ref, feats_ref, out_ref, count_ref):
    rows = feats_ref.shape[0]
    blocks = rows // LANES
    groups, contract = code_ref.shape
    high = code_ref[...] >> 7
    low = code_ref[...] & (LANES - 1)
    tall = lax.broadcasted_iota(jnp.int32, (blocks * part, contract), 0)
    short = lax.broadcasted_iota(jnp.int32, (LANES, contract), 0)
    for g in range(groups):
        left = one_hot(tall == high[g : g + 1, :])
        right = one_hot(short == low[g : g + 1, :])
        counts = lax.dot_general(
            left, right, (((1,), (1,)), ((), ())), preferred_element_type=jnp.float32
        ).astype(jnp.bfloat16)
        for b in range(blocks):
            count_ref[g * part : (g + 1) * part, b * LANES : (b + 1) * LANES] = counts[
                b * part : (b + 1) * part, :
            ]
    out_ref[...] = jnp.dot(count_ref[...], feats_ref[...], preferred_element_type=jnp.float32)


def local_sums(feats, neighbours, length):
    rows, width = feats.shape
    slots = neighbours.shape[1]
    part = 2 * LANES // slots
    used = jnp.arange(slots, dtype=jnp.int32)[None, :] < length[:, None]
    place = (jnp.arange(rows, dtype=jnp.int32) % part)[:, None]
    high = (neighbours // LANES) * part + place
    code = jnp.where(used, high * LANES + neighbours % LANES, -1).reshape(-1, part * slots)
    groups = 16
    return pl.pallas_call(
        lambda *refs: local_body(part, *refs),
        grid=(rows // (groups * part),),
        in_specs=[
            pl.BlockSpec((groups, part * slots), lambda i: (i, 0)),
            pl.BlockSpec((rows, width), lambda i: (0, 0)),
        ],
        out_specs=pl.BlockSpec((groups * part, width), lambda i: (i, 0)),
        out_shape=jax.ShapeDtypeStruct((rows, width), jnp.float32),
        scratch_shapes=[pltpu.VMEM((groups * part, rows), jnp.bfloat16)],
        compiler_params=pltpu.CompilerParams(vmem_limit_bytes=14 * MIB),
        cost_estimate=pl.CostEstimate(
            flops=10 * rows * rows * width, bytes_accessed=4 * rows * width, transcendentals=0
        ),
        name="local_sums",
    )(code, feats)


def load_table(sources, stage, table, sem):
    copies = []
    start = 0
    for source in sources:
        count = source.shape[0]
        size = min(count, CHUNK)
        for first in range(0, count, size):
            copies.append(
                pltpu.make_async_copy(
                    source.at[pl.ds(first, size)],
                    stage.at[pl.ds(start, size)],
                    sem.at[len(copies)],
                )
            )
            start += size
    for copy in copies:
        copy.start()
    table[2 * start : 2 * start + 8, :] = jnp.zeros((8, LANES), jnp.float32)
    start = 0
    for copy in copies:
        copy.wait()
        size = copy.dst_ref.shape[0]

        def widen(i, carry, first=start):
            at = first + i * WIDEN
            block = stage[pl.ds(pl.multiple_of(at, WIDEN), WIDEN), :].astype(jnp.float32)
            table[pl.ds(2 * at, WIDEN, stride=2), :] = block[:, :LANES]
            table[pl.ds(2 * at + 1, WIDEN, stride=2), :] = block[:, LANES:]
            return carry

        lax.fori_loop(0, size // WIDEN, widen, 0)
        start += size


def chunk_count(sources):
    return sum(-(-source.shape[0] // CHUNK) for source in sources)


def add_rows(index_ref, table, out_ref, slots, unroll):
    def step(i, carry):
        base = (i * unroll // LANES) * (slots * LANES) + i * unroll % LANES
        for u in range(unroll):
            v = i * unroll + u
            total = None
            for k in range(slots):
                at = index_ref[base + k * LANES + u]
                row = table[pl.ds(pl.multiple_of(at, 2), 2), :]
                total = row if total is None else total + row
            out_ref[pl.ds(pl.multiple_of(2 * v, 2), 2), :] = total
        return carry

    lax.fori_loop(0, out_ref.shape[0] // (2 * unroll), step, 0)


def fetch(pairs, sem):
    copies = [
        pltpu.make_async_copy(source, target, sem.at[i]) for i, (source, target) in enumerate(pairs)
    ]
    for copy in copies:
        copy.start()
    return copies


def halves(ref, start, size):
    return [ref[pl.ds(2 * start + h, size, stride=2), :] for h in range(2)]


def list_body(slots, pieces, index_hbm, loc_hbm, *refs):
    sources, (out_ref, index, loc, stage, table, sem, extra) = refs[:pieces], refs[pieces:]
    ready, later = fetch([(index_hbm, index), (loc_hbm, loc)], extra)
    load_table(sources, stage, table, sem)
    ready.wait()
    add_rows(index, table, out_ref, slots, UNROLL)
    later.wait()

    def merge(i, carry):
        start = pl.multiple_of(i * WIDEN, WIDEN)
        for h, part in enumerate(halves(out_ref, start, WIDEN)):
            own = loc[pl.ds(start, WIDEN), h * LANES : (h + 1) * LANES]
            out_ref[pl.ds(2 * start + h, WIDEN, stride=2), :] = part + own
        return carry

    lax.fori_loop(0, loc.shape[0] // WIDEN, merge, 0)


def row_index(neighbours, length, count):
    used = jnp.arange(neighbours.shape[1], dtype=jnp.int32)[None, :] < length[:, None]
    rows, slots = neighbours.shape
    index = jnp.where(used, neighbours * 2, 2 * count).T.reshape(slots, rows // LANES, LANES)
    return index.transpose(1, 0, 2).reshape(-1)


def list_sums(index, slots, sources, loc):
    width = sources[0].shape[1]
    count = sum(source.shape[0] for source in sources)
    rows = index.shape[0] // slots
    return pl.pallas_call(
        lambda *refs: list_body(slots, len(sources), *refs),
        in_specs=[pl.BlockSpec(memory_space=pltpu.HBM)] * (2 + len(sources)),
        out_specs=pl.BlockSpec(memory_space=pltpu.VMEM),
        out_shape=pltpu.HBM((2 * rows, LANES), jnp.float32),
        scratch_shapes=[
            pltpu.SMEM(index.shape, index.dtype),
            pltpu.VMEM(loc.shape, loc.dtype),
            pltpu.VMEM((count, width), sources[0].dtype),
            pltpu.VMEM((2 * count + 8, LANES), jnp.float32),
            pltpu.SemaphoreType.DMA((chunk_count(sources),)),
            pltpu.SemaphoreType.DMA((2,)),
        ],
        compiler_params=pltpu.CompilerParams(vmem_limit_bytes=34 * MIB),
        cost_estimate=pl.CostEstimate(
            flops=20_000_000_000, bytes_accessed=2 * count * width, transcendentals=0
        ),
        name="list_sums",
    )(index, loc, *sources)


def layer_body(slots, pieces, index_hbm, *refs):
    sources, refs = refs[:pieces], refs[pieces:]
    outside, (bias_ref, out_ref), refs = refs[:4], refs[4:6], refs[6:]
    index, inside, (stage, table, last, sem, extra) = refs[0], refs[1:5], refs[5:]
    ready, *later = fetch([(index_hbm, index), *zip(outside, inside)], extra)
    load_table(sources, stage, table, sem)
    ready.wait()
    add_rows(index, table, last, slots, UNROLL)
    for copy in later:
        copy.wait()
    partial, degree, feats, weight = inside
    rows, width = feats.shape

    def finish(i, carry):
        start = pl.multiple_of(i * WIDEN, WIDEN)
        span = pl.ds(start, WIDEN)
        divisor = degree[span, :]
        means = [
            ((mine + theirs) / divisor).astype(jnp.bfloat16)
            for mine, theirs in zip(halves(partial, start, WIDEN), halves(last, start, WIDEN))
        ]
        result = jnp.dot(feats[span, :], weight[:width, :], preferred_element_type=jnp.float32)
        result += jnp.dot(
            jnp.concatenate(means, axis=1), weight[width:, :], preferred_element_type=jnp.float32
        )
        result += bias_ref[...]
        out_ref[span, :] = jnp.maximum(result, 0.0).astype(out_ref.dtype)
        return carry

    lax.fori_loop(0, rows // WIDEN, finish, 0)


def layer(index, slots, sources, partial, degree, feats, weight, bias):
    width = sources[0].shape[1]
    count = sum(source.shape[0] for source in sources)
    rows = feats.shape[0]
    outside = [partial, degree, feats, weight]
    vmem = pl.BlockSpec(memory_space=pltpu.VMEM)
    return pl.pallas_call(
        lambda *refs: layer_body(slots, len(sources), *refs),
        in_specs=[pl.BlockSpec(memory_space=pltpu.HBM)] * (1 + len(sources) + len(outside)) + [vmem],
        out_specs=vmem,
        out_shape=jax.ShapeDtypeStruct((rows, width), feats.dtype),
        scratch_shapes=[pltpu.SMEM(index.shape, index.dtype)]
        + [pltpu.VMEM(array.shape, array.dtype) for array in outside]
        + [
            pltpu.VMEM((count, width), feats.dtype),
            pltpu.VMEM((2 * count + 8, LANES), jnp.float32),
            pltpu.VMEM((2 * rows, LANES), jnp.float32),
            pltpu.SemaphoreType.DMA((chunk_count(sources),)),
            pltpu.SemaphoreType.DMA((1 + len(outside),)),
        ],
        compiler_params=pltpu.CompilerParams(vmem_limit_bytes=30 * MIB),
        cost_estimate=pl.CostEstimate(
            flops=20_000_000_000, bytes_accessed=2 * count * width, transcendentals=0
        ),
        name="layer",
    )(index, *sources, *outside, bias)


RING = 4
STRIDES = {"x": 32, "z": 8, "y": 2}
ORDERS = (("y", "z", "x"), ("z", "x", "y"))


def moved(stage, step):
    pairs = []
    for device in range(2 * RING**3):
        stride = STRIDES[ORDERS[device % 2][stage]]
        at = device // stride % RING
        pairs.append((device, device + (step(at) - at) * stride))
    return pairs


def swapped(block):
    return lax.ppermute(block, "dom", [(device, device ^ 1) for device in range(2 * RING**3)])


def gray(value):
    return value ^ (value >> 1)


def hub_place(hub, rows_each):
    me = lax.axis_index("dom")
    device = hub // rows_each
    apart = {
        name: ((device // stride % RING), (me // stride % RING)) for name, stride in STRIDES.items()
    }
    near = {name: gray(theirs ^ mine) for name, (theirs, mine) in apart.items()}
    far = {name: gray((theirs - mine) & (RING - 1)) for name, (theirs, mine) in apart.items()}
    core = device & 1

    def place(order):
        return (far[order[2]] * RING + near[order[1]]) * RING + near[order[0]]

    block = jnp.where(core == 0, place(ORDERS[0]), place(ORDERS[1]))
    block += (core ^ (me & 1)) * RING**3
    return block * rows_each + hub % rows_each


def per_device(
    feats, hub_feat, weight, bias, loc_nbr, loc_len, hub_nbr, hub_len, send_list, halo_nbr, halo_len
):
    rows, width = feats.shape
    peers, slots = send_list.shape
    each = hub_feat.shape[0]

    block, outgoing, piece = hub_feat, None, 0
    for stage in range(2):
        for flip in (1, 3):
            other = lax.ppermute(block, "dom", moved(stage, lambda i, flip=flip: i ^ flip))
            outgoing = gather_to_send(feats, send_list, piece, 4, outgoing)
            block = jnp.concatenate([block, other], axis=0)
            block, outgoing = lax.optimization_barrier((block, outgoing))
            piece += 1
    hubs = [block] + [
        lax.ppermute(block, "dom", moved(2, lambda i, shift=shift: (i - shift) % RING))
        for shift in (1, 3, 2)
    ]
    arrived = lax.all_to_all(
        outgoing.reshape(peers, slots, width), "dom", split_axis=0, concat_axis=0, tiled=True
    ).reshape(peers * slots, width)
    loc = local_sums(feats, loc_nbr, loc_len)
    hub_index = row_index(hub_place(hub_nbr, each), hub_len, peers * each)
    halo_index = row_index(halo_nbr, halo_len, peers * slots)
    hubs, loc, hub_index, halo_index = lax.optimization_barrier((hubs, loc, hub_index, halo_index))
    hubs = hubs + [swapped(part) for part in hubs]
    partial = list_sums(hub_index, hub_nbr.shape[1], hubs, loc)
    degree = jnp.broadcast_to(
        (loc_len + hub_len + halo_len).astype(jnp.float32)[:, None], (rows, LANES)
    )
    return layer(
        halo_index, halo_nbr.shape[1], [arrived], partial, degree, feats, weight, bias[None, :]
    )


def solution(mesh):
    placed = (
        P("dom", None),
        P("dom", None),
        P(),
        P(),
        P("dom", None),
        P("dom"),
        P("dom", None),
        P("dom"),
        P("dom", None),
        P("dom", None),
        P("dom"),
    )
    return jax.shard_map(
        per_device, mesh=mesh, in_specs=placed, out_specs=P("dom", None), check_vma=False
    )
```

```python
import jax
import jax.numpy as jnp
from jax import lax
from jax.experimental import pallas as pl
from jax.experimental.pallas import tpu as pltpu
from jax.sharding import PartitionSpec as P

LANES = 128
MIB = 2**20
CHUNK = 1024
WIDEN = 256
UNROLL = 32
SEND_PEERS = 16
SEND_TURNS = ((0, 3), (3, 5))


def one_hot(mask):
    return jnp.where(mask, 1.0, 0.0).astype(jnp.bfloat16)


def widen_rows(source, first, table, start, size):
    def step(i, carry):
        at = start + i * WIDEN
        block = source[pl.ds(pl.multiple_of(first + i * WIDEN, WIDEN), WIDEN), :]
        block = block.astype(jnp.float32)
        table[pl.ds(2 * at, WIDEN, stride=2), :] = block[:, :LANES]
        table[pl.ds(2 * at + 1, WIDEN, stride=2), :] = block[:, LANES:]
        return carry

    lax.fori_loop(0, size // WIDEN, step, 0)


def send_body(first, slots, index_hbm, feats_ref, out_ref, index, table, stage, sem):
    step = pl.program_id(0)

    @pl.when(step == 0)
    def _():
        copy = pltpu.make_async_copy(index_hbm, index, sem)
        copy.start()
        widen_rows(feats_ref, 0, table, 0, feats_ref.shape[0])
        copy.wait()

    here = out_ref.shape[0] // slots
    peers = index.shape[0] // slots

    def gather(buffer, peer):
        at = first + step * here + peer
        for s in range(slots):
            row = table[pl.ds(pl.multiple_of(index[s * peers + at], 2), 2), :]
            stage[pl.ds(2 * (buffer * slots + s), 2), :] = row

    def pack(buffer, peer):
        both = [stage[pl.ds(2 * buffer * slots + h, slots, stride=2), :] for h in range(2)]
        rows = jnp.concatenate(both, axis=1).astype(out_ref.dtype)
        out_ref[pl.ds(pl.multiple_of(peer * slots, slots), slots), :] = rows

    gather(0, 0)

    def pair(i, carry):
        peer = 2 * i
        pack(0, peer)
        gather(1, peer + 1)
        pack(1, peer + 1)
        gather(0, jnp.minimum(peer + 2, here - 1))
        return carry

    lax.fori_loop(0, here // 2, pair, 0)


def gather_to_send(feats, index, slots, part, so_far):
    rows, width = feats.shape
    count = index.shape[0]
    group = SEND_PEERS * slots
    first, steps = part
    inputs = [index, feats]
    in_specs = [
        pl.BlockSpec(memory_space=pl.ANY),
        pl.BlockSpec((rows, width), lambda i: (0, 0)),
    ]
    aliases = {}
    if so_far is not None:
        inputs.append(so_far)
        in_specs.append(pl.BlockSpec(memory_space=pltpu.HBM))
        aliases = {2: 0}
    return pl.pallas_call(
        lambda index_hbm, feats_ref, *refs: send_body(
            SEND_PEERS * first, slots, index_hbm, feats_ref, *refs[-5:]
        ),
        grid=(steps,),
        in_specs=in_specs,
        out_specs=pl.BlockSpec((group, width), lambda i: (first + i, 0)),
        out_shape=pltpu.HBM((count, width), feats.dtype),
        scratch_shapes=[
            pltpu.SMEM(index.shape, index.dtype),
            pltpu.VMEM((2 * rows, LANES), jnp.float32),
            pltpu.VMEM((4 * slots, LANES), jnp.float32),
            pltpu.SemaphoreType.DMA,
        ],
        input_output_aliases=aliases,
        compiler_params=pltpu.CompilerParams(vmem_limit_bytes=14 * MIB),
        cost_estimate=pl.CostEstimate(
            flops=4 * group * steps * rows * width,
            bytes_accessed=2 * group * steps * width,
            transcendentals=0,
        ),
        name="gather_to_send",
    )(*inputs)


def local_body(part, code_ref, feats_ref, out_ref, count_ref):
    rows = feats_ref.shape[0]
    blocks = rows // LANES
    groups, contract = code_ref.shape
    high = code_ref[...] >> 7
    low = code_ref[...] & (LANES - 1)
    tall = lax.broadcasted_iota(jnp.int32, (blocks * part, contract), 0)
    short = lax.broadcasted_iota(jnp.int32, (LANES, contract), 0)
    for g in range(groups):
        left = one_hot(tall == high[g : g + 1, :])
        right = one_hot(short == low[g : g + 1, :])
        counts = lax.dot_general(
            left, right, (((1,), (1,)), ((), ())), preferred_element_type=jnp.float32
        ).astype(jnp.bfloat16)
        for b in range(blocks):
            count_ref[g * part : (g + 1) * part, b * LANES : (b + 1) * LANES] = counts[
                b * part : (b + 1) * part, :
            ]
    out_ref[...] = jnp.dot(count_ref[...], feats_ref[...], preferred_element_type=jnp.float32)


def local_sums(feats, neighbours, length):
    rows, width = feats.shape
    slots = neighbours.shape[1]
    part = 2 * LANES // slots
    used = jnp.arange(slots, dtype=jnp.int32)[None, :] < length[:, None]
    place = (jnp.arange(rows, dtype=jnp.int32) % part)[:, None]
    high = (neighbours // LANES) * part + place
    code = jnp.where(used, high * LANES + neighbours % LANES, -1).reshape(-1, part * slots)
    groups = 16
    return pl.pallas_call(
        lambda *refs: local_body(part, *refs),
        grid=(rows // (groups * part),),
        in_specs=[
            pl.BlockSpec((groups, part * slots), lambda i: (i, 0)),
            pl.BlockSpec((rows, width), lambda i: (0, 0)),
        ],
        out_specs=pl.BlockSpec((groups * part, width), lambda i: (i, 0)),
        out_shape=jax.ShapeDtypeStruct((rows, width), jnp.float32),
        scratch_shapes=[pltpu.VMEM((groups * part, rows), jnp.bfloat16)],
        compiler_params=pltpu.CompilerParams(vmem_limit_bytes=14 * MIB),
        cost_estimate=pl.CostEstimate(
            flops=4 * rows * rows * width, bytes_accessed=4 * rows * width, transcendentals=0
        ),
        name="local_sums",
    )(code, feats)


def start_table(sources, stage, sem):
    copies = []
    start = 0
    for source in sources:
        size = min(source.shape[0], CHUNK)
        for first in range(0, source.shape[0], size):
            copy = pltpu.make_async_copy(
                source.at[pl.ds(first, size)], stage.at[pl.ds(start, size)], sem.at[len(copies)]
            )
            copy.start()
            copies.append((copy, start, size))
            start += size
    return copies


def finish_table(copies, stage, table):
    count = stage.shape[0]
    table[2 * count : 2 * count + 8, :] = jnp.zeros((8, LANES), jnp.float32)
    for copy, start, size in copies:
        copy.wait()
        widen_rows(stage, start, table, start, size)


def chunk_count(sources):
    return sum(-(-source.shape[0] // CHUNK) for source in sources)


def add_rows(index_ref, table, out_ref, slots, unroll):
    def step(i, carry):
        base = (i * unroll // LANES) * (slots * LANES) + i * unroll % LANES
        for u in range(unroll):
            v = i * unroll + u
            total = None
            for k in range(slots):
                at = index_ref[base + k * LANES + u]
                row = table[pl.ds(pl.multiple_of(at, 2), 2), :]
                total = row if total is None else total + row
            out_ref[pl.ds(pl.multiple_of(2 * v, 2), 2), :] = total
        return carry

    lax.fori_loop(0, out_ref.shape[0] // (2 * unroll), step, 0)


def fetch(pairs, sem):
    copies = [
        pltpu.make_async_copy(source, target, sem.at[i]) for i, (source, target) in enumerate(pairs)
    ]
    for copy in copies:
        copy.start()
    return copies


def halves(ref, start, size):
    return [ref[pl.ds(2 * start + h, size, stride=2), :] for h in range(2)]


def list_body(slots, pieces, index_hbm, loc_hbm, *refs):
    sources, (out_ref, index, loc, stage, table, sem, extra) = refs[:pieces], refs[pieces:]
    copies = start_table(sources, stage, sem)
    ready, later = fetch([(index_hbm, index), (loc_hbm, loc)], extra)
    finish_table(copies, stage, table)
    ready.wait()
    add_rows(index, table, out_ref, slots, UNROLL)
    later.wait()

    def merge(i, carry):
        start = pl.multiple_of(i * WIDEN, WIDEN)
        for h, part in enumerate(halves(out_ref, start, WIDEN)):
            own = loc[pl.ds(start, WIDEN), h * LANES : (h + 1) * LANES]
            out_ref[pl.ds(2 * start + h, WIDEN, stride=2), :] = part + own
        return carry

    lax.fori_loop(0, loc.shape[0] // WIDEN, merge, 0)


def row_index(neighbours, length, count):
    used = jnp.arange(neighbours.shape[1], dtype=jnp.int32)[None, :] < length[:, None]
    rows, slots = neighbours.shape
    index = jnp.where(used, neighbours * 2, 2 * count).T.reshape(slots, rows // LANES, LANES)
    return index.transpose(1, 0, 2).reshape(-1)


def list_sums(index, slots, sources, loc):
    width = sources[0].shape[1]
    count = sum(source.shape[0] for source in sources)
    rows = index.shape[0] // slots
    return pl.pallas_call(
        lambda *refs: list_body(slots, len(sources), *refs),
        in_specs=[pl.BlockSpec(memory_space=pltpu.HBM)] * (2 + len(sources)),
        out_specs=pl.BlockSpec(memory_space=pltpu.VMEM),
        out_shape=pltpu.HBM((2 * rows, LANES), jnp.float32),
        scratch_shapes=[
            pltpu.SMEM(index.shape, index.dtype),
            pltpu.VMEM(loc.shape, loc.dtype),
            pltpu.VMEM((count, width), sources[0].dtype),
            pltpu.VMEM((2 * count + 8, LANES), jnp.float32),
            pltpu.SemaphoreType.DMA((chunk_count(sources),)),
            pltpu.SemaphoreType.DMA((2,)),
        ],
        compiler_params=pltpu.CompilerParams(vmem_limit_bytes=34 * MIB),
        cost_estimate=pl.CostEstimate(
            flops=27_000_000_000, bytes_accessed=2 * count * width, transcendentals=0
        ),
        name="list_sums",
    )(index, loc, *sources)


def layer_body(slots, pieces, index_hbm, *refs):
    sources, refs = refs[:pieces], refs[pieces:]
    outside, (bias_ref, out_ref), refs = refs[:4], refs[4:6], refs[6:]
    index, inside, (stage, table, last, sem, extra) = refs[0], refs[1:5], refs[5:]
    copies = start_table(sources, stage, sem)
    ready, *later = fetch([(index_hbm, index), *zip(outside, inside)], extra)
    finish_table(copies, stage, table)
    ready.wait()
    add_rows(index, table, last, slots, UNROLL)
    for copy in later:
        copy.wait()
    partial, degree, feats, weight = inside
    rows, width = feats.shape

    def finish(i, carry):
        start = pl.multiple_of(i * WIDEN, WIDEN)
        span = pl.ds(start, WIDEN)
        divisor = degree[span, :]
        means = [
            ((mine + theirs) / divisor).astype(jnp.bfloat16)
            for mine, theirs in zip(halves(partial, start, WIDEN), halves(last, start, WIDEN))
        ]
        result = jnp.dot(feats[span, :], weight[:width, :], preferred_element_type=jnp.float32)
        result += jnp.dot(
            jnp.concatenate(means, axis=1), weight[width:, :], preferred_element_type=jnp.float32
        )
        result += bias_ref[...]
        out_ref[span, :] = jnp.maximum(result, 0.0).astype(out_ref.dtype)
        return carry

    lax.fori_loop(0, rows // WIDEN, finish, 0)


def layer(index, slots, sources, partial, degree, feats, weight, bias):
    width = sources[0].shape[1]
    count = sum(source.shape[0] for source in sources)
    rows = feats.shape[0]
    outside = [partial, degree, feats, weight]
    vmem = pl.BlockSpec(memory_space=pltpu.VMEM)
    return pl.pallas_call(
        lambda *refs: layer_body(slots, len(sources), *refs),
        in_specs=[pl.BlockSpec(memory_space=pltpu.HBM)] * (1 + len(sources) + len(outside)) + [vmem],
        out_specs=vmem,
        out_shape=jax.ShapeDtypeStruct((rows, width), feats.dtype),
        scratch_shapes=[pltpu.SMEM(index.shape, index.dtype)]
        + [pltpu.VMEM(array.shape, array.dtype) for array in outside]
        + [
            pltpu.VMEM((count, width), feats.dtype),
            pltpu.VMEM((2 * count + 8, LANES), jnp.float32),
            pltpu.VMEM((2 * rows, LANES), jnp.float32),
            pltpu.SemaphoreType.DMA((chunk_count(sources),)),
            pltpu.SemaphoreType.DMA((1 + len(outside),)),
        ],
        compiler_params=pltpu.CompilerParams(vmem_limit_bytes=62 * MIB),
        cost_estimate=pl.CostEstimate(
            flops=27_000_000_000, bytes_accessed=2 * count * width, transcendentals=0
        ),
        name="layer",
    )(index, *sources, *outside, bias)


RING = 4
STRIDES = {"x": 32, "z": 8, "y": 2}
ORDERS = (("y", "z", "x"), ("z", "x", "y"))


def moved(stage, step):
    pairs = []
    for device in range(2 * RING**3):
        stride = STRIDES[ORDERS[device % 2][stage]]
        at = device // stride % RING
        pairs.append((device, device + (step(at) - at) * stride))
    return pairs


def swapped(block):
    return lax.ppermute(block, "dom", [(device, device ^ 1) for device in range(2 * RING**3)])


def gray(value):
    return value ^ (value >> 1)


def hub_place(hub, rows_each):
    me = lax.axis_index("dom")
    device = hub // rows_each
    apart = {
        name: ((device // stride % RING), (me // stride % RING)) for name, stride in STRIDES.items()
    }
    apart = {name: (theirs - mine) & (RING - 1) for name, (theirs, mine) in apart.items()}
    core = device & 1

    def place(order):
        return (gray(apart[order[2]]) * RING + apart[order[1]]) * RING + apart[order[0]]

    block = jnp.where(core == 0, place(ORDERS[0]), place(ORDERS[1]))
    block += (core ^ (me & 1)) * RING**3
    return block * rows_each + hub % rows_each


def along(block, stage, shifts):
    return [
        lax.ppermute(block, "dom", moved(stage, lambda i, shift=shift: (i - shift) % RING))
        for shift in shifts
    ]


def per_device(
    feats, hub_feat, weight, bias, loc_nbr, loc_len, hub_nbr, hub_len, send_list, halo_nbr, halo_len
):
    rows, width = feats.shape
    peers, slots = send_list.shape
    each = hub_feat.shape[0]

    send_index = send_list.T.reshape(-1) * 2
    block = jnp.concatenate([hub_feat] + along(hub_feat, 0, (1, 2, 3)), axis=0)
    block, send_index = lax.optimization_barrier((block, send_index))
    others = along(block, 1, (1, 2, 3))
    outgoing = gather_to_send(feats, send_index, slots, SEND_TURNS[0], None)
    block = jnp.concatenate([block] + others, axis=0)
    block, outgoing = lax.optimization_barrier((block, outgoing))
    hubs = [block] + along(block, 2, (1, 3, 2))
    outgoing = gather_to_send(feats, send_index, slots, SEND_TURNS[1], outgoing)
    outgoing, loc_nbr = lax.optimization_barrier((outgoing, loc_nbr))
    arrived = lax.all_to_all(
        outgoing.reshape(peers, slots, width), "dom", split_axis=0, concat_axis=0, tiled=True
    ).reshape(peers * slots, width)
    loc = local_sums(feats, loc_nbr, loc_len)
    hub_index = row_index(hub_place(hub_nbr, each), hub_len, peers * each)
    halo_index = row_index(halo_nbr, halo_len, peers * slots)
    degree = jnp.broadcast_to(
        (loc_len + hub_len + halo_len).astype(jnp.float32)[:, None], (rows, LANES)
    )
    hubs, loc, hub_index, halo_index, degree = lax.optimization_barrier(
        (hubs, loc, hub_index, halo_index, degree)
    )
    hubs = hubs + [swapped(part) for part in hubs]
    partial = list_sums(hub_index, hub_nbr.shape[1], hubs, loc)
    return layer(
        halo_index, halo_nbr.shape[1], [arrived], partial, degree, feats, weight, bias[None, :]
    )


def solution(mesh):
    placed = (
        P("dom", None),
        P("dom", None),
        P(),
        P(),
        P("dom", None),
        P("dom"),
        P("dom", None),
        P("dom"),
        P("dom", None),
        P("dom", None),
        P("dom"),
    )
    return jax.shard_map(
        per_device, mesh=mesh, in_specs=placed, out_specs=P("dom", None), check_vma=False
    )
```

```python
import jax
import jax.numpy as jnp
from jax import lax
from jax.experimental import pallas as pl
from jax.experimental.pallas import tpu as pltpu
from jax.sharding import PartitionSpec as P

LANES = 128
MIB = 2**20
CHUNK = 1024
WIDEN = 256
UNROLL = 32
SEND_PEERS = 16
SEND_TURNS = ((0, 3), (3, 5))


def one_hot(mask):
    return jnp.where(mask, 1.0, 0.0).astype(jnp.bfloat16)


def widen_rows(source, first, table, start, size):
    def step(i, carry):
        at = start + i * WIDEN
        block = source[pl.ds(pl.multiple_of(first + i * WIDEN, WIDEN), WIDEN), :]
        block = block.astype(jnp.float32)
        table[pl.ds(2 * at, WIDEN, stride=2), :] = block[:, :LANES]
        table[pl.ds(2 * at + 1, WIDEN, stride=2), :] = block[:, LANES:]
        return carry

    lax.fori_loop(0, size // WIDEN, step, 0)


def send_body(first, slots, index_hbm, feats_ref, out_ref, index, table, stage, sem):
    step = pl.program_id(0)

    @pl.when(step == 0)
    def _():
        copy = pltpu.make_async_copy(index_hbm, index, sem)
        copy.start()
        widen_rows(feats_ref, 0, table, 0, feats_ref.shape[0])
        copy.wait()

    here = out_ref.shape[0] // slots
    peers = index.shape[0] // slots

    def gather(buffer, peer):
        at = first + step * here + peer
        for s in range(slots):
            row = table[pl.ds(pl.multiple_of(index[s * peers + at], 2), 2), :]
            stage[pl.ds(2 * (buffer * slots + s), 2), :] = row

    def pack(buffer, peer):
        both = [stage[pl.ds(2 * buffer * slots + h, slots, stride=2), :] for h in range(2)]
        rows = jnp.concatenate(both, axis=1).astype(out_ref.dtype)
        out_ref[pl.ds(pl.multiple_of(peer * slots, slots), slots), :] = rows

    gather(0, 0)

    def pair(i, carry):
        peer = 2 * i
        pack(0, peer)
        gather(1, peer + 1)
        pack(1, peer + 1)
        gather(0, jnp.minimum(peer + 2, here - 1))
        return carry

    lax.fori_loop(0, here // 2, pair, 0)


def gather_to_send(feats, index, slots, part, so_far):
    rows, width = feats.shape
    count = index.shape[0]
    group = SEND_PEERS * slots
    first, steps = part
    inputs = [index, feats]
    in_specs = [
        pl.BlockSpec(memory_space=pl.ANY),
        pl.BlockSpec((rows, width), lambda i: (0, 0)),
    ]
    aliases = {}
    if so_far is not None:
        inputs.append(so_far)
        in_specs.append(pl.BlockSpec(memory_space=pltpu.HBM))
        aliases = {2: 0}
    return pl.pallas_call(
        lambda index_hbm, feats_ref, *refs: send_body(
            SEND_PEERS * first, slots, index_hbm, feats_ref, *refs[-5:]
        ),
        grid=(steps,),
        in_specs=in_specs,
        out_specs=pl.BlockSpec((group, width), lambda i: (first + i, 0)),
        out_shape=pltpu.HBM((count, width), feats.dtype),
        scratch_shapes=[
            pltpu.SMEM(index.shape, index.dtype),
            pltpu.VMEM((2 * rows, LANES), jnp.float32),
            pltpu.VMEM((4 * slots, LANES), jnp.float32),
            pltpu.SemaphoreType.DMA,
        ],
        input_output_aliases=aliases,
        compiler_params=pltpu.CompilerParams(vmem_limit_bytes=14 * MIB),
        cost_estimate=pl.CostEstimate(
            flops=4 * group * steps * rows * width,
            bytes_accessed=2 * group * steps * width,
            transcendentals=0,
        ),
        name="gather_to_send",
    )(*inputs)


def local_body(part, code_ref, feats_ref, out_ref, count_ref):
    rows = feats_ref.shape[0]
    blocks = rows // LANES
    groups, contract = code_ref.shape
    high = code_ref[...] >> 7
    low = code_ref[...] & (LANES - 1)
    tall = lax.broadcasted_iota(jnp.int32, (blocks * part, contract), 0)
    short = lax.broadcasted_iota(jnp.int32, (LANES, contract), 0)
    for g in range(groups):
        left = one_hot(tall == high[g : g + 1, :])
        right = one_hot(short == low[g : g + 1, :])
        counts = lax.dot_general(
            left, right, (((1,), (1,)), ((), ())), preferred_element_type=jnp.float32
        ).astype(jnp.bfloat16)
        for b in range(blocks):
            count_ref[g * part : (g + 1) * part, b * LANES : (b + 1) * LANES] = counts[
                b * part : (b + 1) * part, :
            ]
    out_ref[...] = jnp.dot(count_ref[...], feats_ref[...], preferred_element_type=jnp.float32)


def local_sums(feats, neighbours, length):
    rows, width = feats.shape
    slots = neighbours.shape[1]
    part = 2 * LANES // slots
    used = jnp.arange(slots, dtype=jnp.int32)[None, :] < length[:, None]
    place = (jnp.arange(rows, dtype=jnp.int32) % part)[:, None]
    high = (neighbours // LANES) * part + place
    code = jnp.where(used, high * LANES + neighbours % LANES, -1).reshape(-1, part * slots)
    groups = 16
    return pl.pallas_call(
        lambda *refs: local_body(part, *refs),
        grid=(rows // (groups * part),),
        in_specs=[
            pl.BlockSpec((groups, part * slots), lambda i: (i, 0)),
            pl.BlockSpec((rows, width), lambda i: (0, 0)),
        ],
        out_specs=pl.BlockSpec((groups * part, width), lambda i: (i, 0)),
        out_shape=jax.ShapeDtypeStruct((rows, width), jnp.float32),
        scratch_shapes=[pltpu.VMEM((groups * part, rows), jnp.bfloat16)],
        compiler_params=pltpu.CompilerParams(vmem_limit_bytes=14 * MIB),
        cost_estimate=pl.CostEstimate(
            flops=4 * rows * rows * width, bytes_accessed=4 * rows * width, transcendentals=0
        ),
        name="local_sums",
    )(code, feats)


def start_table(sources, stage, sem):
    copies = []
    start = 0
    for source in sources:
        size = min(source.shape[0], CHUNK)
        for first in range(0, source.shape[0], size):
            copy = pltpu.make_async_copy(
                source.at[pl.ds(first, size)], stage.at[pl.ds(start, size)], sem.at[len(copies)]
            )
            copy.start()
            copies.append((copy, start, size))
            start += size
    return copies


def finish_table(copies, stage, table):
    count = stage.shape[0]
    table[2 * count : 2 * count + 8, :] = jnp.zeros((8, LANES), jnp.float32)
    for copy, start, size in copies:
        copy.wait()
        widen_rows(stage, start, table, start, size)


def chunk_count(sources):
    return sum(-(-source.shape[0] // CHUNK) for source in sources)


def add_rows(index_ref, table, out_ref, slots, unroll):
    def step(i, carry):
        base = (i * unroll // LANES) * (slots * LANES) + i * unroll % LANES
        for u in range(unroll):
            v = i * unroll + u
            total = None
            for k in range(slots):
                at = index_ref[base + k * LANES + u]
                row = table[pl.ds(pl.multiple_of(at, 2), 2), :]
                total = row if total is None else total + row
            out_ref[pl.ds(pl.multiple_of(2 * v, 2), 2), :] = total
        return carry

    lax.fori_loop(0, out_ref.shape[0] // (2 * unroll), step, 0)


def fetch(pairs, sem, first=0):
    copies = [
        pltpu.make_async_copy(source, target, sem.at[first + i])
        for i, (source, target) in enumerate(pairs)
    ]
    for copy in copies:
        copy.start()
    return copies


def halves(ref, start, size):
    return [ref[pl.ds(2 * start + h, size, stride=2), :] for h in range(2)]


def list_body(slots, pieces, index_hbm, loc_hbm, *refs):
    sources, (out_ref, index, loc, stage, table, sem, extra) = refs[:pieces], refs[pieces:]
    copies = start_table(sources, stage, sem)
    (ready,) = fetch([(index_hbm, index)], extra)
    finish_table(copies, stage, table)
    (later,) = fetch([(loc_hbm, loc)], extra, 1)
    ready.wait()
    add_rows(index, table, out_ref, slots, UNROLL)
    later.wait()

    def merge(i, carry):
        start = pl.multiple_of(i * WIDEN, WIDEN)
        for h, part in enumerate(halves(out_ref, start, WIDEN)):
            own = loc[pl.ds(start, WIDEN), h * LANES : (h + 1) * LANES]
            out_ref[pl.ds(2 * start + h, WIDEN, stride=2), :] = part + own
        return carry

    lax.fori_loop(0, loc.shape[0] // WIDEN, merge, 0)


def row_index(neighbours, length, count):
    used = jnp.arange(neighbours.shape[1], dtype=jnp.int32)[None, :] < length[:, None]
    rows, slots = neighbours.shape
    index = jnp.where(used, neighbours * 2, 2 * count).T.reshape(slots, rows // LANES, LANES)
    return index.transpose(1, 0, 2).reshape(-1)


def list_sums(index, slots, sources, loc):
    width = sources[0].shape[1]
    count = sum(source.shape[0] for source in sources)
    rows = index.shape[0] // slots
    return pl.pallas_call(
        lambda *refs: list_body(slots, len(sources), *refs),
        in_specs=[pl.BlockSpec(memory_space=pltpu.HBM)] * (2 + len(sources)),
        out_specs=pl.BlockSpec(memory_space=pltpu.VMEM),
        out_shape=pltpu.HBM((2 * rows, LANES), jnp.float32),
        scratch_shapes=[
            pltpu.SMEM(index.shape, index.dtype),
            pltpu.VMEM(loc.shape, loc.dtype),
            pltpu.VMEM((count, width), sources[0].dtype),
            pltpu.VMEM((2 * count + 8, LANES), jnp.float32),
            pltpu.SemaphoreType.DMA((chunk_count(sources),)),
            pltpu.SemaphoreType.DMA((2,)),
        ],
        compiler_params=pltpu.CompilerParams(vmem_limit_bytes=34 * MIB),
        cost_estimate=pl.CostEstimate(
            flops=27_000_000_000, bytes_accessed=2 * count * width, transcendentals=0
        ),
        name="list_sums",
    )(index, loc, *sources)


def layer_body(slots, pieces, index_hbm, *refs):
    sources, refs = refs[:pieces], refs[pieces:]
    outside, (bias_ref, out_hbm), refs = refs[:4], refs[4:6], refs[6:]
    index, inside, (out_ref, stage, table, last, sem, extra, out_sem) = refs[0], refs[1:5], refs[5:]
    copies = start_table(sources, stage, sem)
    (ready,) = fetch([(index_hbm, index)], extra)
    finish_table(copies, stage, table)
    later = fetch(list(zip(outside, inside)), extra, 1)
    ready.wait()
    add_rows(index, table, last, slots, UNROLL)
    for copy in later:
        copy.wait()
    partial, degree, feats, weight = inside
    rows, width = feats.shape

    writes = []
    for i in range(rows // WIDEN):
        start = i * WIDEN
        span = pl.ds(start, WIDEN)
        divisor = degree[span, :]
        means = [
            ((mine + theirs) / divisor).astype(jnp.bfloat16)
            for mine, theirs in zip(halves(partial, start, WIDEN), halves(last, start, WIDEN))
        ]
        result = jnp.dot(feats[span, :], weight[:width, :], preferred_element_type=jnp.float32)
        result += jnp.dot(
            jnp.concatenate(means, axis=1), weight[width:, :], preferred_element_type=jnp.float32
        )
        result += bias_ref[...]
        out_ref[span, :] = jnp.maximum(result, 0.0).astype(out_ref.dtype)
        writes += fetch([(out_ref.at[span], out_hbm.at[span])], out_sem, i)
    for write in writes:
        write.wait()


def layer(index, slots, sources, partial, degree, feats, weight, bias):
    width = sources[0].shape[1]
    count = sum(source.shape[0] for source in sources)
    rows = feats.shape[0]
    outside = [partial, degree, feats, weight]
    vmem = pl.BlockSpec(memory_space=pltpu.VMEM)
    return pl.pallas_call(
        lambda *refs: layer_body(slots, len(sources), *refs),
        in_specs=[pl.BlockSpec(memory_space=pltpu.HBM)] * (1 + len(sources) + len(outside)) + [vmem],
        out_specs=pl.BlockSpec(memory_space=pltpu.HBM),
        out_shape=pltpu.HBM((rows, width), feats.dtype),
        scratch_shapes=[pltpu.SMEM(index.shape, index.dtype)]
        + [pltpu.VMEM(array.shape, array.dtype) for array in outside]
        + [
            pltpu.VMEM((rows, width), feats.dtype),
            pltpu.VMEM((count, width), feats.dtype),
            pltpu.VMEM((2 * count + 8, LANES), jnp.float32),
            pltpu.VMEM((2 * rows, LANES), jnp.float32),
            pltpu.SemaphoreType.DMA((chunk_count(sources),)),
            pltpu.SemaphoreType.DMA((1 + len(outside),)),
            pltpu.SemaphoreType.DMA((rows // WIDEN,)),
        ],
        compiler_params=pltpu.CompilerParams(vmem_limit_bytes=62 * MIB),
        cost_estimate=pl.CostEstimate(
            flops=27_000_000_000, bytes_accessed=2 * count * width, transcendentals=0
        ),
        name="layer",
    )(index, *sources, *outside, bias)


RING = 4
STRIDES = {"x": 32, "z": 8, "y": 2}
ORDERS = (("y", "z", "x"), ("z", "x", "y"))


def moved(stage, step):
    pairs = []
    for device in range(2 * RING**3):
        stride = STRIDES[ORDERS[device % 2][stage]]
        at = device // stride % RING
        pairs.append((device, device + (step(at) - at) * stride))
    return pairs


def swapped(block):
    return lax.ppermute(block, "dom", [(device, device ^ 1) for device in range(2 * RING**3)])


def gray(value):
    return value ^ (value >> 1)


def hub_place(hub, rows_each):
    me = lax.axis_index("dom")
    device = hub // rows_each
    apart = {
        name: ((device // stride % RING), (me // stride % RING)) for name, stride in STRIDES.items()
    }
    apart = {name: (theirs - mine) & (RING - 1) for name, (theirs, mine) in apart.items()}
    core = device & 1

    def place(order):
        return (gray(apart[order[2]]) * RING + apart[order[1]]) * RING + apart[order[0]]

    block = jnp.where(core == 0, place(ORDERS[0]), place(ORDERS[1]))
    block += (core ^ (me & 1)) * RING**3
    return block * rows_each + hub % rows_each


def along(block, stage, shifts):
    return [
        lax.ppermute(block, "dom", moved(stage, lambda i, shift=shift: (i - shift) % RING))
        for shift in shifts
    ]


def per_device(
    feats, hub_feat, weight, bias, loc_nbr, loc_len, hub_nbr, hub_len, send_list, halo_nbr, halo_len
):
    rows, width = feats.shape
    peers, slots = send_list.shape
    each = hub_feat.shape[0]

    send_index = send_list.T.reshape(-1) * 2
    block = jnp.concatenate([hub_feat] + along(hub_feat, 0, (1, 2, 3)), axis=0)
    block, send_index = lax.optimization_barrier((block, send_index))
    others = along(block, 1, (1, 2, 3))
    outgoing = gather_to_send(feats, send_index, slots, SEND_TURNS[0], None)
    block = jnp.concatenate([block] + others, axis=0)
    block, outgoing = lax.optimization_barrier((block, outgoing))
    hubs = [block] + along(block, 2, (1, 3, 2))
    outgoing = gather_to_send(feats, send_index, slots, SEND_TURNS[1], outgoing)
    outgoing, loc_nbr = lax.optimization_barrier((outgoing, loc_nbr))
    arrived = lax.all_to_all(
        outgoing.reshape(peers, slots, width), "dom", split_axis=0, concat_axis=0, tiled=True
    ).reshape(peers * slots, width)
    loc = local_sums(feats, loc_nbr, loc_len)
    hub_index = row_index(hub_place(hub_nbr, each), hub_len, peers * each)
    halo_index = row_index(halo_nbr, halo_len, peers * slots)
    degree = jnp.broadcast_to(
        (loc_len + hub_len + halo_len).astype(jnp.float32)[:, None], (rows, LANES)
    )
    hubs, loc, hub_index, halo_index, degree = lax.optimization_barrier(
        (hubs, loc, hub_index, halo_index, degree)
    )
    hubs = hubs + [swapped(part) for part in hubs]
    partial = list_sums(hub_index, hub_nbr.shape[1], hubs, loc)
    return layer(
        halo_index, halo_nbr.shape[1], [arrived], partial, degree, feats, weight, bias[None, :]
    )


def solution(mesh):
    placed = (
        P("dom", None),
        P("dom", None),
        P(),
        P(),
        P("dom", None),
        P("dom"),
        P("dom", None),
        P("dom"),
        P("dom", None),
        P("dom", None),
        P("dom"),
    )
    return jax.shard_map(
        per_device, mesh=mesh, in_specs=placed, out_specs=P("dom", None), check_vma=False
    )
```

```python
import jax
import jax.numpy as jnp
from jax import lax
from jax.experimental import pallas as pl
from jax.experimental.pallas import tpu as pltpu
from jax.sharding import PartitionSpec as P

LANES = 128
MIB = 2**20
CHUNK = 1024
WIDEN = 256
UNROLL = 64
SEND_PEERS = 16
SEND_TURNS = ((0, 3), (3, 5))


def one_hot(mask):
    return jnp.where(mask, 1.0, 0.0).astype(jnp.bfloat16)


def widen_rows(source, first, table, start, size):
    def step(i, carry):
        at = start + i * WIDEN
        block = source[pl.ds(pl.multiple_of(first + i * WIDEN, WIDEN), WIDEN), :]
        block = block.astype(jnp.float32)
        table[pl.ds(2 * at, WIDEN, stride=2), :] = block[:, :LANES]
        table[pl.ds(2 * at + 1, WIDEN, stride=2), :] = block[:, LANES:]
        return carry

    lax.fori_loop(0, size // WIDEN, step, 0)


def send_body(first, slots, index_hbm, feats_ref, out_ref, index, table, stage, sem):
    step = pl.program_id(0)

    @pl.when(step == 0)
    def _():
        copy = pltpu.make_async_copy(index_hbm, index, sem)
        copy.start()
        widen_rows(feats_ref, 0, table, 0, feats_ref.shape[0])
        copy.wait()

    here = out_ref.shape[0] // slots
    peers = index.shape[0] // slots

    def gather(buffer, peer):
        at = first + step * here + peer
        for s in range(slots):
            row = table[pl.ds(pl.multiple_of(index[s * peers + at], 2), 2), :]
            stage[pl.ds(2 * (buffer * slots + s), 2), :] = row

    def pack(buffer, peer):
        both = [stage[pl.ds(2 * buffer * slots + h, slots, stride=2), :] for h in range(2)]
        rows = jnp.concatenate(both, axis=1).astype(out_ref.dtype)
        out_ref[pl.ds(pl.multiple_of(peer * slots, slots), slots), :] = rows

    gather(0, 0)

    def pair(i, carry):
        peer = 2 * i
        pack(0, peer)
        gather(1, peer + 1)
        pack(1, peer + 1)
        gather(0, jnp.minimum(peer + 2, here - 1))
        return carry

    lax.fori_loop(0, here // 2, pair, 0)


def gather_to_send(feats, index, slots, part, so_far):
    rows, width = feats.shape
    count = index.shape[0]
    group = SEND_PEERS * slots
    first, steps = part
    inputs = [index, feats]
    in_specs = [
        pl.BlockSpec(memory_space=pl.ANY),
        pl.BlockSpec((rows, width), lambda i: (0, 0)),
    ]
    aliases = {}
    if so_far is not None:
        inputs.append(so_far)
        in_specs.append(pl.BlockSpec(memory_space=pltpu.HBM))
        aliases = {2: 0}
    return pl.pallas_call(
        lambda index_hbm, feats_ref, *refs: send_body(
            SEND_PEERS * first, slots, index_hbm, feats_ref, *refs[-5:]
        ),
        grid=(steps,),
        in_specs=in_specs,
        out_specs=pl.BlockSpec((group, width), lambda i: (first + i, 0)),
        out_shape=pltpu.HBM((count, width), feats.dtype),
        scratch_shapes=[
            pltpu.SMEM(index.shape, index.dtype),
            pltpu.VMEM((2 * rows, LANES), jnp.float32),
            pltpu.VMEM((4 * slots, LANES), jnp.float32),
            pltpu.SemaphoreType.DMA,
        ],
        input_output_aliases=aliases,
        compiler_params=pltpu.CompilerParams(vmem_limit_bytes=14 * MIB),
        cost_estimate=pl.CostEstimate(
            flops=4 * group * steps * rows * width,
            bytes_accessed=2 * group * steps * width,
            transcendentals=0,
        ),
        name="gather_to_send",
    )(*inputs)


def local_body(part, code_ref, feats_ref, out_ref, count_ref):
    rows = feats_ref.shape[0]
    blocks = rows // LANES
    groups, contract = code_ref.shape
    high = code_ref[...] >> 7
    low = code_ref[...] & (LANES - 1)
    tall = lax.broadcasted_iota(jnp.int32, (blocks * part, contract), 0)
    short = lax.broadcasted_iota(jnp.int32, (LANES, contract), 0)
    for g in range(groups):
        left = one_hot(tall == high[g : g + 1, :])
        right = one_hot(short == low[g : g + 1, :])
        counts = lax.dot_general(
            left, right, (((1,), (1,)), ((), ())), preferred_element_type=jnp.float32
        ).astype(jnp.bfloat16)
        for b in range(blocks):
            count_ref[g * part : (g + 1) * part, b * LANES : (b + 1) * LANES] = counts[
                b * part : (b + 1) * part, :
            ]
    out_ref[...] = jnp.dot(count_ref[...], feats_ref[...], preferred_element_type=jnp.float32)


def local_sums(feats, neighbours, length):
    rows, width = feats.shape
    slots = neighbours.shape[1]
    part = 2 * LANES // slots
    used = jnp.arange(slots, dtype=jnp.int32)[None, :] < length[:, None]
    place = (jnp.arange(rows, dtype=jnp.int32) % part)[:, None]
    high = (neighbours // LANES) * part + place
    code = jnp.where(used, high * LANES + neighbours % LANES, -1).reshape(-1, part * slots)
    groups = 16
    return pl.pallas_call(
        lambda *refs: local_body(part, *refs),
        grid=(rows // (groups * part),),
        in_specs=[
            pl.BlockSpec((groups, part * slots), lambda i: (i, 0)),
            pl.BlockSpec((rows, width), lambda i: (0, 0)),
        ],
        out_specs=pl.BlockSpec((groups * part, width), lambda i: (i, 0)),
        out_shape=jax.ShapeDtypeStruct((rows, width), jnp.float32),
        scratch_shapes=[pltpu.VMEM((groups * part, rows), jnp.bfloat16)],
        compiler_params=pltpu.CompilerParams(vmem_limit_bytes=14 * MIB),
        cost_estimate=pl.CostEstimate(
            flops=4 * rows * rows * width, bytes_accessed=4 * rows * width, transcendentals=0
        ),
        name="local_sums",
    )(code, feats)


def start_table(sources, stage, sem):
    copies = []
    start = 0
    for source in sources:
        size = min(source.shape[0], CHUNK)
        for first in range(0, source.shape[0], size):
            copy = pltpu.make_async_copy(
                source.at[pl.ds(first, size)], stage.at[pl.ds(start, size)], sem.at[len(copies)]
            )
            copy.start()
            copies.append((copy, start, size))
            start += size
    return copies


def finish_table(copies, stage, table):
    count = stage.shape[0]
    table[2 * count : 2 * count + 8, :] = jnp.zeros((8, LANES), jnp.float32)
    for copy, start, size in copies:
        copy.wait()
        widen_rows(stage, start, table, start, size)


def chunk_count(sources):
    return sum(-(-source.shape[0] // CHUNK) for source in sources)


def add_rows(index_ref, table, out_ref, slots, unroll):
    def step(i, carry):
        base = (i * unroll // LANES) * (slots * LANES) + i * unroll % LANES
        for u in range(unroll):
            v = i * unroll + u
            total = None
            for k in range(slots):
                at = index_ref[base + k * LANES + u]
                row = table[pl.ds(pl.multiple_of(at, 2), 2), :]
                total = row if total is None else total + row
            out_ref[pl.ds(pl.multiple_of(2 * v, 2), 2), :] = total
        return carry

    lax.fori_loop(0, out_ref.shape[0] // (2 * unroll), step, 0)


def fetch(pairs, sem, first=0):
    copies = [
        pltpu.make_async_copy(source, target, sem.at[first + i])
        for i, (source, target) in enumerate(pairs)
    ]
    for copy in copies:
        copy.start()
    return copies


def halves(ref, start, size):
    return [ref[pl.ds(2 * start + h, size, stride=2), :] for h in range(2)]


def list_body(slots, pieces, index_hbm, loc_hbm, *refs):
    sources, (out_ref, index, loc, stage, table, sem, extra) = refs[:pieces], refs[pieces:]
    copies = start_table(sources, stage, sem)
    (ready,) = fetch([(index_hbm, index)], extra)
    finish_table(copies, stage, table)
    (later,) = fetch([(loc_hbm, loc)], extra, 1)
    ready.wait()
    add_rows(index, table, out_ref, slots, UNROLL)
    later.wait()

    def merge(i, carry):
        start = pl.multiple_of(i * WIDEN, WIDEN)
        for h, part in enumerate(halves(out_ref, start, WIDEN)):
            own = loc[pl.ds(start, WIDEN), h * LANES : (h + 1) * LANES]
            out_ref[pl.ds(2 * start + h, WIDEN, stride=2), :] = part + own
        return carry

    lax.fori_loop(0, loc.shape[0] // WIDEN, merge, 0)


def row_index(neighbours, length, count):
    used = jnp.arange(neighbours.shape[1], dtype=jnp.int32)[None, :] < length[:, None]
    rows, slots = neighbours.shape
    index = jnp.where(used, neighbours * 2, 2 * count).T.reshape(slots, rows // LANES, LANES)
    return index.transpose(1, 0, 2).reshape(-1)


def list_sums(index, slots, sources, loc):
    width = sources[0].shape[1]
    count = sum(source.shape[0] for source in sources)
    rows = index.shape[0] // slots
    return pl.pallas_call(
        lambda *refs: list_body(slots, len(sources), *refs),
        in_specs=[pl.BlockSpec(memory_space=pltpu.HBM)] * (2 + len(sources)),
        out_specs=pl.BlockSpec(memory_space=pltpu.VMEM),
        out_shape=pltpu.HBM((2 * rows, LANES), jnp.float32),
        scratch_shapes=[
            pltpu.SMEM(index.shape, index.dtype),
            pltpu.VMEM(loc.shape, loc.dtype),
            pltpu.VMEM((count, width), sources[0].dtype),
            pltpu.VMEM((2 * count + 8, LANES), jnp.float32),
            pltpu.SemaphoreType.DMA((chunk_count(sources),)),
            pltpu.SemaphoreType.DMA((2,)),
        ],
        compiler_params=pltpu.CompilerParams(vmem_limit_bytes=34 * MIB),
        cost_estimate=pl.CostEstimate(
            flops=27_000_000_000, bytes_accessed=2 * count * width, transcendentals=0
        ),
        name="list_sums",
    )(index, loc, *sources)


def layer_body(slots, pieces, index_hbm, *refs):
    sources, refs = refs[:pieces], refs[pieces:]
    outside, out_hbm, refs = refs[:4], refs[4], refs[5:]
    index, inside, (out_ref, stage, table, last, sem, extra, out_sem) = refs[0], refs[1:5], refs[5:]
    copies = start_table(sources, stage, sem)
    (ready,) = fetch([(index_hbm, index)], extra)
    finish_table(copies, stage, table)
    later = fetch(list(zip(outside, inside)), extra, 1)
    ready.wait()
    add_rows(index, table, last, slots, UNROLL)
    for copy in later:
        copy.wait()
    partial, degree, base, weight = inside
    rows = base.shape[0]

    writes = []
    for i in range(rows // WIDEN):
        start = i * WIDEN
        span = pl.ds(start, WIDEN)
        divisor = degree[span, :]
        means = [
            ((mine + theirs) / divisor).astype(jnp.bfloat16)
            for mine, theirs in zip(halves(partial, start, WIDEN), halves(last, start, WIDEN))
        ]
        result = base[span, :] + jnp.dot(
            jnp.concatenate(means, axis=1), weight[...], preferred_element_type=jnp.float32
        )
        out_ref[span, :] = jnp.maximum(result, 0.0).astype(out_ref.dtype)
        writes += fetch([(out_ref.at[span], out_hbm.at[span])], out_sem, i)
    for write in writes:
        write.wait()


def layer(index, slots, sources, partial, degree, base, weight):
    width = sources[0].shape[1]
    count = sum(source.shape[0] for source in sources)
    rows = base.shape[0]
    outside = [partial, degree, base, weight]
    return pl.pallas_call(
        lambda *refs: layer_body(slots, len(sources), *refs),
        in_specs=[pl.BlockSpec(memory_space=pltpu.HBM)] * (1 + len(sources) + len(outside)),
        out_specs=pl.BlockSpec(memory_space=pltpu.HBM),
        out_shape=pltpu.HBM((rows, width), sources[0].dtype),
        scratch_shapes=[pltpu.SMEM(index.shape, index.dtype)]
        + [pltpu.VMEM(array.shape, array.dtype) for array in outside]
        + [
            pltpu.VMEM((rows, width), sources[0].dtype),
            pltpu.VMEM((count, width), sources[0].dtype),
            pltpu.VMEM((2 * count + 8, LANES), jnp.float32),
            pltpu.VMEM((2 * rows, LANES), jnp.float32),
            pltpu.SemaphoreType.DMA((chunk_count(sources),)),
            pltpu.SemaphoreType.DMA((1 + len(outside),)),
            pltpu.SemaphoreType.DMA((rows // WIDEN,)),
        ],
        compiler_params=pltpu.CompilerParams(vmem_limit_bytes=62 * MIB),
        cost_estimate=pl.CostEstimate(
            flops=27_000_000_000, bytes_accessed=2 * count * width, transcendentals=0
        ),
        name="layer",
    )(index, *sources, *outside)


RING = 4
STRIDES = {"x": 32, "z": 8, "y": 2}
ORDERS = (("y", "z", "x"), ("z", "x", "y"))


def moved(stage, step):
    pairs = []
    for device in range(2 * RING**3):
        stride = STRIDES[ORDERS[device % 2][stage]]
        at = device // stride % RING
        pairs.append((device, device + (step(at) - at) * stride))
    return pairs


def swapped(block):
    return lax.ppermute(block, "dom", [(device, device ^ 1) for device in range(2 * RING**3)])


def gray(value):
    return value ^ (value >> 1)


def hub_place(hub, rows_each):
    me = lax.axis_index("dom")
    device = hub // rows_each
    apart = {
        name: ((device // stride % RING), (me // stride % RING)) for name, stride in STRIDES.items()
    }
    apart = {name: (theirs - mine) & (RING - 1) for name, (theirs, mine) in apart.items()}
    core = device & 1

    def place(order):
        return (gray(apart[order[2]]) * RING + apart[order[1]]) * RING + apart[order[0]]

    block = jnp.where(core == 0, place(ORDERS[0]), place(ORDERS[1]))
    block += (core ^ (me & 1)) * RING**3
    return block * rows_each + hub % rows_each


def along(block, stage, shifts):
    return [
        lax.ppermute(block, "dom", moved(stage, lambda i, shift=shift: (i - shift) % RING))
        for shift in shifts
    ]


def per_device(
    feats, hub_feat, weight, bias, loc_nbr, loc_len, hub_nbr, hub_len, send_list, halo_nbr, halo_len
):
    rows, width = feats.shape
    peers, slots = send_list.shape
    each = hub_feat.shape[0]

    send_index = send_list.T.reshape(-1) * 2
    block = jnp.concatenate([hub_feat] + along(hub_feat, 0, (1, 2, 3)), axis=0)
    block, send_index = lax.optimization_barrier((block, send_index))
    others = along(block, 1, (1, 2, 3))
    outgoing = gather_to_send(feats, send_index, slots, SEND_TURNS[0], None)
    block = jnp.concatenate([block] + others, axis=0)
    block, outgoing = lax.optimization_barrier((block, outgoing))
    hubs = [block] + along(block, 2, (1, 3, 2))
    outgoing = gather_to_send(feats, send_index, slots, SEND_TURNS[1], outgoing)
    outgoing, loc_nbr = lax.optimization_barrier((outgoing, loc_nbr))
    arrived = lax.all_to_all(
        outgoing.reshape(peers, slots, width), "dom", split_axis=0, concat_axis=0, tiled=True
    ).reshape(peers * slots, width)
    loc = local_sums(feats, loc_nbr, loc_len)
    hub_index = row_index(hub_place(hub_nbr, each), hub_len, peers * each)
    halo_index = row_index(halo_nbr, halo_len, peers * slots)
    degree = jnp.broadcast_to(
        (loc_len + hub_len + halo_len).astype(jnp.float32)[:, None], (rows, LANES)
    )
    base = jnp.dot(feats, weight[:width], preferred_element_type=jnp.float32) + bias
    hubs, loc, hub_index, halo_index, degree, base = lax.optimization_barrier(
        (hubs, loc, hub_index, halo_index, degree, base)
    )
    hubs = hubs + [swapped(part) for part in hubs]
    partial = list_sums(hub_index, hub_nbr.shape[1], hubs, loc)
    return layer(
        halo_index, halo_nbr.shape[1], [arrived], partial, degree, base, weight[width:]
    )


def solution(mesh):
    placed = (
        P("dom", None),
        P("dom", None),
        P(),
        P(),
        P("dom", None),
        P("dom"),
        P("dom", None),
        P("dom"),
        P("dom", None),
        P("dom", None),
        P("dom"),
    )
    return jax.shard_map(
        per_device, mesh=mesh, in_specs=placed, out_specs=P("dom", None), check_vma=False
    )
```

```python
import jax
import jax.numpy as jnp
from jax import lax
from jax.experimental import pallas as pl
from jax.experimental.pallas import tpu as pltpu
from jax.sharding import PartitionSpec as P

LANES = 128
MIB = 2**20
CHUNK = 1024
WIDEN = 256
UNROLL = 32
SEND_PEERS = 16
SEND_TURNS = ((0, 3), (3, 5))


def one_hot(mask):
    return jnp.where(mask, 1.0, 0.0).astype(jnp.bfloat16)


def widen_rows(source, first, table, start, size):
    def step(i, carry):
        at = start + i * WIDEN
        block = source[pl.ds(pl.multiple_of(first + i * WIDEN, WIDEN), WIDEN), :]
        block = block.astype(jnp.float32)
        table[pl.ds(2 * at, WIDEN, stride=2), :] = block[:, :LANES]
        table[pl.ds(2 * at + 1, WIDEN, stride=2), :] = block[:, LANES:]
        return carry

    lax.fori_loop(0, size // WIDEN, step, 0)


def send_body(first, slots, index_hbm, feats_ref, out_ref, index, table, stage, sem):
    step = pl.program_id(0)

    @pl.when(step == 0)
    def _():
        copy = pltpu.make_async_copy(index_hbm, index, sem)
        copy.start()
        widen_rows(feats_ref, 0, table, 0, feats_ref.shape[0])
        copy.wait()

    here = out_ref.shape[0] // slots
    peers = index.shape[0] // slots

    def gather(buffer, peer):
        at = first + step * here + peer
        for s in range(slots):
            row = table[pl.ds(pl.multiple_of(index[s * peers + at], 2), 2), :]
            stage[pl.ds(2 * (buffer * slots + s), 2), :] = row

    def pack(buffer, peer):
        both = [stage[pl.ds(2 * buffer * slots + h, slots, stride=2), :] for h in range(2)]
        rows = jnp.concatenate(both, axis=1).astype(out_ref.dtype)
        out_ref[pl.ds(pl.multiple_of(peer * slots, slots), slots), :] = rows

    gather(0, 0)

    def pair(i, carry):
        peer = 2 * i
        pack(0, peer)
        gather(1, peer + 1)
        pack(1, peer + 1)
        gather(0, jnp.minimum(peer + 2, here - 1))
        return carry

    lax.fori_loop(0, here // 2, pair, 0)


def gather_to_send(feats, index, slots, part, so_far):
    rows, width = feats.shape
    count = index.shape[0]
    group = SEND_PEERS * slots
    first, steps = part
    inputs = [index, feats]
    in_specs = [
        pl.BlockSpec(memory_space=pl.ANY),
        pl.BlockSpec((rows, width), lambda i: (0, 0)),
    ]
    aliases = {}
    if so_far is not None:
        inputs.append(so_far)
        in_specs.append(pl.BlockSpec(memory_space=pltpu.HBM))
        aliases = {2: 0}
    return pl.pallas_call(
        lambda index_hbm, feats_ref, *refs: send_body(
            SEND_PEERS * first, slots, index_hbm, feats_ref, *refs[-5:]
        ),
        grid=(steps,),
        in_specs=in_specs,
        out_specs=pl.BlockSpec((group, width), lambda i: (first + i, 0)),
        out_shape=pltpu.HBM((count, width), feats.dtype),
        scratch_shapes=[
            pltpu.SMEM(index.shape, index.dtype),
            pltpu.VMEM((2 * rows, LANES), jnp.float32),
            pltpu.VMEM((4 * slots, LANES), jnp.float32),
            pltpu.SemaphoreType.DMA,
        ],
        input_output_aliases=aliases,
        compiler_params=pltpu.CompilerParams(vmem_limit_bytes=14 * MIB),
        cost_estimate=pl.CostEstimate(
            flops=4 * group * steps * rows * width,
            bytes_accessed=2 * group * steps * width,
            transcendentals=0,
        ),
        name="gather_to_send",
    )(*inputs)


def local_body(part, code_ref, feats_ref, out_ref, count_ref):
    rows = feats_ref.shape[0]
    blocks = rows // LANES
    groups, contract = code_ref.shape
    high = code_ref[...] >> 7
    low = code_ref[...] & (LANES - 1)
    tall = lax.broadcasted_iota(jnp.int32, (blocks * part, contract), 0)
    short = lax.broadcasted_iota(jnp.int32, (LANES, contract), 0)
    for g in range(groups):
        left = one_hot(tall == high[g : g + 1, :])
        right = one_hot(short == low[g : g + 1, :])
        counts = lax.dot_general(
            left, right, (((1,), (1,)), ((), ())), preferred_element_type=jnp.float32
        ).astype(jnp.bfloat16)
        for b in range(blocks):
            count_ref[g * part : (g + 1) * part, b * LANES : (b + 1) * LANES] = counts[
                b * part : (b + 1) * part, :
            ]
    out_ref[...] = jnp.dot(count_ref[...], feats_ref[...], preferred_element_type=jnp.float32)


def local_sums(feats, neighbours, length):
    rows, width = feats.shape
    slots = neighbours.shape[1]
    part = 2 * LANES // slots
    used = jnp.arange(slots, dtype=jnp.int32)[None, :] < length[:, None]
    place = (jnp.arange(rows, dtype=jnp.int32) % part)[:, None]
    high = (neighbours // LANES) * part + place
    code = jnp.where(used, high * LANES + neighbours % LANES, -1).reshape(-1, part * slots)
    groups = 16
    return pl.pallas_call(
        lambda *refs: local_body(part, *refs),
        grid=(rows // (groups * part),),
        in_specs=[
            pl.BlockSpec((groups, part * slots), lambda i: (i, 0)),
            pl.BlockSpec((rows, width), lambda i: (0, 0)),
        ],
        out_specs=pl.BlockSpec((groups * part, width), lambda i: (i, 0)),
        out_shape=jax.ShapeDtypeStruct((rows, width), jnp.float32),
        scratch_shapes=[pltpu.VMEM((groups * part, rows), jnp.bfloat16)],
        compiler_params=pltpu.CompilerParams(vmem_limit_bytes=14 * MIB),
        cost_estimate=pl.CostEstimate(
            flops=4 * rows * rows * width, bytes_accessed=4 * rows * width, transcendentals=0
        ),
        name="local_sums",
    )(code, feats)


def start_table(sources, stage, sem):
    copies = []
    start = 0
    for source in sources:
        size = min(source.shape[0], CHUNK)
        for first in range(0, source.shape[0], size):
            copy = pltpu.make_async_copy(
                source.at[pl.ds(first, size)], stage.at[pl.ds(start, size)], sem.at[len(copies)]
            )
            copy.start()
            copies.append((copy, start, size))
            start += size
    return copies


def finish_table(copies, stage, table):
    count = stage.shape[0]
    table[2 * count : 2 * count + 8, :] = jnp.zeros((8, LANES), jnp.float32)
    for copy, start, size in copies:
        copy.wait()
        widen_rows(stage, start, table, start, size)


def chunk_count(sources):
    return sum(-(-source.shape[0] // CHUNK) for source in sources)


def add_rows(index_ref, table, out_ref, slots, unroll):
    def step(i, carry):
        base = (i * unroll // LANES) * (slots * LANES) + i * unroll % LANES
        for u in range(unroll):
            v = i * unroll + u
            total = None
            for k in range(slots):
                at = index_ref[base + k * LANES + u]
                row = table[pl.ds(pl.multiple_of(at, 2), 2), :]
                total = row if total is None else total + row
            out_ref[pl.ds(pl.multiple_of(2 * v, 2), 2), :] = total
        return carry

    lax.fori_loop(0, out_ref.shape[0] // (2 * unroll), step, 0)


def fetch(pairs, sem, first=0):
    copies = [
        pltpu.make_async_copy(source, target, sem.at[first + i])
        for i, (source, target) in enumerate(pairs)
    ]
    for copy in copies:
        copy.start()
    return copies


def halves(ref, start, size):
    return [ref[pl.ds(2 * start + h, size, stride=2), :] for h in range(2)]


def list_body(slots, pieces, index_hbm, loc_hbm, *refs):
    sources, (out_ref, index, loc, stage, table, sem, extra) = refs[:pieces], refs[pieces:]
    copies = start_table(sources, stage, sem)
    (ready,) = fetch([(index_hbm, index)], extra)
    finish_table(copies, stage, table)
    (later,) = fetch([(loc_hbm, loc)], extra, 1)
    ready.wait()
    add_rows(index, table, out_ref, slots, UNROLL)
    later.wait()

    def merge(i, carry):
        start = pl.multiple_of(i * WIDEN, WIDEN)
        for h, part in enumerate(halves(out_ref, start, WIDEN)):
            own = loc[pl.ds(start, WIDEN), h * LANES : (h + 1) * LANES]
            out_ref[pl.ds(2 * start + h, WIDEN, stride=2), :] = part + own
        return carry

    lax.fori_loop(0, loc.shape[0] // WIDEN, merge, 0)


def row_index(neighbours, length, count):
    used = jnp.arange(neighbours.shape[1], dtype=jnp.int32)[None, :] < length[:, None]
    rows, slots = neighbours.shape
    index = jnp.where(used, neighbours * 2, 2 * count).T.reshape(slots, rows // LANES, LANES)
    return index.transpose(1, 0, 2).reshape(-1)


def list_sums(index, slots, sources, loc):
    width = sources[0].shape[1]
    count = sum(source.shape[0] for source in sources)
    rows = index.shape[0] // slots
    return pl.pallas_call(
        lambda *refs: list_body(slots, len(sources), *refs),
        in_specs=[pl.BlockSpec(memory_space=pltpu.HBM)] * (2 + len(sources)),
        out_specs=pl.BlockSpec(memory_space=pltpu.VMEM),
        out_shape=pltpu.HBM((2 * rows, LANES), jnp.float32),
        scratch_shapes=[
            pltpu.SMEM(index.shape, index.dtype),
            pltpu.VMEM(loc.shape, loc.dtype),
            pltpu.VMEM((count, width), sources[0].dtype),
            pltpu.VMEM((2 * count + 8, LANES), jnp.float32),
            pltpu.SemaphoreType.DMA((chunk_count(sources),)),
            pltpu.SemaphoreType.DMA((2,)),
        ],
        compiler_params=pltpu.CompilerParams(vmem_limit_bytes=34 * MIB),
        cost_estimate=pl.CostEstimate(
            flops=27_000_000_000, bytes_accessed=2 * count * width, transcendentals=0
        ),
        name="list_sums",
    )(index, loc, *sources)


def layer_body(slots, pieces, index_hbm, *refs):
    sources, refs = refs[:pieces], refs[pieces:]
    outside, (bias_ref, out_hbm), refs = refs[:4], refs[4:6], refs[6:]
    index, inside, (out_ref, stage, table, last, sem, extra, out_sem) = refs[0], refs[1:5], refs[5:]
    copies = start_table(sources, stage, sem)
    (ready,) = fetch([(index_hbm, index)], extra)
    finish_table(copies, stage, table)
    later = fetch(list(zip(outside, inside)), extra, 1)
    ready.wait()
    add_rows(index, table, last, slots, UNROLL)
    for copy in later:
        copy.wait()
    partial, degree, feats, weight = inside
    rows, width = feats.shape

    writes = []
    for i in range(rows // WIDEN):
        start = i * WIDEN
        span = pl.ds(start, WIDEN)
        divisor = degree[span, :]
        means = [
            ((mine + theirs) / divisor).astype(jnp.bfloat16)
            for mine, theirs in zip(halves(partial, start, WIDEN), halves(last, start, WIDEN))
        ]
        result = jnp.dot(feats[span, :], weight[:width, :], preferred_element_type=jnp.float32)
        result += jnp.dot(
            jnp.concatenate(means, axis=1), weight[width:, :], preferred_element_type=jnp.float32
        )
        result += bias_ref[...]
        out_ref[span, :] = jnp.maximum(result, 0.0).astype(out_ref.dtype)
        writes += fetch([(out_ref.at[span], out_hbm.at[span])], out_sem, i)
    for write in writes:
        write.wait()


def layer(index, slots, sources, partial, degree, feats, weight, bias):
    width = sources[0].shape[1]
    count = sum(source.shape[0] for source in sources)
    rows = feats.shape[0]
    outside = [partial, degree, feats, weight]
    vmem = pl.BlockSpec(memory_space=pltpu.VMEM)
    return pl.pallas_call(
        lambda *refs: layer_body(slots, len(sources), *refs),
        in_specs=[pl.BlockSpec(memory_space=pltpu.HBM)] * (1 + len(sources) + len(outside)) + [vmem],
        out_specs=pl.BlockSpec(memory_space=pltpu.HBM),
        out_shape=pltpu.HBM((rows, width), feats.dtype),
        scratch_shapes=[pltpu.SMEM(index.shape, index.dtype)]
        + [pltpu.VMEM(array.shape, array.dtype) for array in outside]
        + [
            pltpu.VMEM((rows, width), feats.dtype),
            pltpu.VMEM((count, width), feats.dtype),
            pltpu.VMEM((2 * count + 8, LANES), jnp.float32),
            pltpu.VMEM((2 * rows, LANES), jnp.float32),
            pltpu.SemaphoreType.DMA((chunk_count(sources),)),
            pltpu.SemaphoreType.DMA((1 + len(outside),)),
            pltpu.SemaphoreType.DMA((rows // WIDEN,)),
        ],
        compiler_params=pltpu.CompilerParams(vmem_limit_bytes=62 * MIB),
        cost_estimate=pl.CostEstimate(
            flops=27_000_000_000, bytes_accessed=2 * count * width, transcendentals=0
        ),
        name="layer",
    )(index, *sources, *outside, bias)


RING = 4
STRIDES = {"x": 32, "z": 8, "y": 2}
ORDERS = (("y", "z", "x"), ("x", "z", "y"))


def moved(stage, step):
    pairs = []
    for device in range(2 * RING**3):
        stride = STRIDES[ORDERS[device % 2][stage]]
        at = device // stride % RING
        pairs.append((device, device + (step(at) - at) * stride))
    return pairs


def swapped(block):
    return lax.ppermute(block, "dom", [(device, device ^ 1) for device in range(2 * RING**3)])


def gray(value):
    return value ^ (value >> 1)


def hub_place(hub, rows_each):
    me = lax.axis_index("dom")
    device = hub // rows_each
    apart = {
        name: ((device // stride % RING), (me // stride % RING)) for name, stride in STRIDES.items()
    }
    apart = {name: (theirs - mine) & (RING - 1) for name, (theirs, mine) in apart.items()}
    core = device & 1

    def place(order):
        return (gray(apart[order[2]]) * RING + apart[order[1]]) * RING + apart[order[0]]

    block = jnp.where(core == 0, place(ORDERS[0]), place(ORDERS[1]))
    block += (core ^ (me & 1)) * RING**3
    return block * rows_each + hub % rows_each


def along(block, stage, shifts):
    return [
        lax.ppermute(block, "dom", moved(stage, lambda i, shift=shift: (i - shift) % RING))
        for shift in shifts
    ]


def per_device(
    feats, hub_feat, weight, bias, loc_nbr, loc_len, hub_nbr, hub_len, send_list, halo_nbr, halo_len
):
    rows, width = feats.shape
    peers, slots = send_list.shape
    each = hub_feat.shape[0]

    send_index = send_list.T.reshape(-1) * 2
    block = jnp.concatenate([hub_feat] + along(hub_feat, 0, (1, 2, 3)), axis=0)
    block, send_index = lax.optimization_barrier((block, send_index))
    others = along(block, 1, (1, 2, 3))
    outgoing = gather_to_send(feats, send_index, slots, SEND_TURNS[0], None)
    block = jnp.concatenate([block] + others, axis=0)
    block, outgoing = lax.optimization_barrier((block, outgoing))
    hubs = [block] + along(block, 2, (1, 3, 2))
    outgoing = gather_to_send(feats, send_index, slots, SEND_TURNS[1], outgoing)
    outgoing, loc_nbr = lax.optimization_barrier((outgoing, loc_nbr))
    arrived = lax.all_to_all(
        outgoing.reshape(peers, slots, width), "dom", split_axis=0, concat_axis=0, tiled=True
    ).reshape(peers * slots, width)
    loc = local_sums(feats, loc_nbr, loc_len)
    hub_index = row_index(hub_place(hub_nbr, each), hub_len, peers * each)
    halo_index = row_index(halo_nbr, halo_len, peers * slots)
    degree = jnp.broadcast_to(
        (loc_len + hub_len + halo_len).astype(jnp.float32)[:, None], (rows, LANES)
    )
    hubs, loc, hub_index, halo_index, degree = lax.optimization_barrier(
        (hubs, loc, hub_index, halo_index, degree)
    )
    hubs = hubs + [swapped(part) for part in hubs]
    partial = list_sums(hub_index, hub_nbr.shape[1], hubs, loc)
    return layer(
        halo_index, halo_nbr.shape[1], [arrived], partial, degree, feats, weight, bias[None, :]
    )


def solution(mesh):
    placed = (
        P("dom", None),
        P("dom", None),
        P(),
        P(),
        P("dom", None),
        P("dom"),
        P("dom", None),
        P("dom"),
        P("dom", None),
        P("dom", None),
        P("dom"),
    )
    return jax.shard_map(
        per_device, mesh=mesh, in_specs=placed, out_specs=P("dom", None), check_vma=False
    )
```
